32 devices in a mesh: space: 8 (over z, y), view: 4 (over x, core).
Axes of the slice: x: 2, y: 2, z: 4, core: 2. Of those that a mesh axis runs over, the one named last changes fastest.
Arguments:
- gaussians: float32 [59, 65536], P(None, 'space'), as said below
- camera_table: float32 [16, 8], replicated, as said below
- view_camera: int32 [4], P('view'), may hold values from 0 to 15
- tile_plan: int32 [4, 128], P('view', 'space'), may hold values from 2204 to 2595, as said below
- requests: int32 [4, 8, 8, 1024], P('view', 'space'), may hold values from 0 to 8191, as said below
- tile_lists: int32 [4, 128, 512], P('view', 'space'), may hold values from 0 to 8191, as said below
- tile_lengths: int32 [4, 128], P('view', 'space'), may hold values from 128 to 512, as said below
- pixel_grad: float32 [4, 128, 3, 256], P('view', 'space'), may hold values from -0.625 to 0.625
Outputs:
- rendered: float32 [4, 128, 3, 256], P('view', 'space')
- gaussian_grad: float32 [59, 65536], P(None, 'space')
The draws below stay inside these ranges and needn't reach their ends.
Inputs may be any that keep to these rules, and one draw needn't show every extreme that they name: `tile_plan`: tile ids count 120 tiles to a row; within a view every tile k < 128 of tile row 18 + floor(k / 32) and tile column 44 + (k mod 32) appears exactly once. `requests`: slots of the owner's 8192 Gaussians; within a view no slot of an owner is requested twice, by one renderer or by two. `tile_lists`: position o * 1024 + k names the k-th slot the renderer requested of owner o; the lists of one renderer's tiles together name each of its requested rows exactly once, each list the same number of rows of every owner, ordered by owner and within an owner by slot; entries from the tile's length on are padding. `tile_lengths`: every view has a tile with all 512 entries live. `camera_table`: quaternion rows lead with 2 to 3 and the rest within 0.3; offsets lie within 0.2 across and 4 to 5 in depth; focal lengths 1.8 to 2.4. `gaussians`: the first quaternion entry lies in 1 to 2.
All inputs are finite; a program needn't handle non-finite values.
Results may differ from the reference program's by a relative error of at most 0.0003.
Values sent between devices are 32-bit elements; how exact they have to be, the bound alone decides.
A program may use at most 256 MiB of HBM per device.

```python
import jax
import jax.numpy as jnp
from jax import lax

PIX = 256
LMAX = 512
CAMS = 16
GDEV = 8192
TILE_DEV = 16
CAP = 1024
VIEWS = 4
TILES_VIEW = 128
N_SPACE = 8


def rotation_rows(quat):
    length = jnp.sqrt(jnp.sum(quat * quat))
    unit_w = quat[0] / length
    unit_x = quat[1] / length
    unit_y = quat[2] / length
    unit_z = quat[3] / length
    return [[1.0 - 2.0 * (unit_y * unit_y + unit_z * unit_z), 2.0 * (unit_x * unit_y - unit_w * unit_z), 2.0 * (unit_x * unit_z + unit_w * unit_y)], [2.0 * (unit_x * unit_y + unit_w * unit_z), 1.0 - 2.0 * (unit_x * unit_x + unit_z * unit_z), 2.0 * (unit_y * unit_z - unit_w * unit_x)], [2.0 * (unit_x * unit_z - unit_w * unit_y), 2.0 * (unit_y * unit_z + unit_w * unit_x), 1.0 - 2.0 * (unit_x * unit_x + unit_y * unit_y)]]


def owner_slots(key):
    key = jax.random.fold_in(key, 301)
    slot_index = jnp.arange(GDEV, dtype=jnp.int32)
    scores = jax.random.randint(key, (N_SPACE, GDEV), 0, 1 << 16) * GDEV + slot_index[None, :]
    scores = jnp.where(slot_index[None, :] == 0, -2, jnp.where(slot_index[None, :] == GDEV - 1, -1, scores))
    return jnp.argsort(scores, axis=1, stable=True).astype(jnp.int32)


def view_tiles(key):
    key = jax.random.fold_in(key, 302)
    tile_index = jnp.arange(TILES_VIEW, dtype=jnp.int32)
    scores = jax.random.randint(key, (VIEWS, TILES_VIEW), 0, 1 << 16) * TILES_VIEW + tile_index[None, :]
    return jnp.argsort(scores, axis=1, stable=True).astype(jnp.int32)


def request_order(key):
    key = jax.random.fold_in(key, 303)
    place_index = jnp.arange(CAP, dtype=jnp.int32)
    scores = jax.random.randint(key, (VIEWS, N_SPACE, N_SPACE, CAP), 0, 1 << 16) * CAP + place_index
    return jnp.argsort(scores, axis=3, stable=True).astype(jnp.int32)


def base_camera(key):
    key = jax.random.fold_in(key, 304)
    keys = jax.random.split(key, 5)
    lead = jax.random.uniform(keys[0], (1,), minval=2.1, maxval=2.9)
    rest = jax.random.uniform(keys[1], (3,), minval=-0.25, maxval=0.25)
    across = jax.random.uniform(keys[2], (2,), minval=-0.15, maxval=0.15)
    depth = jax.random.uniform(keys[3], (1,), minval=4.1, maxval=4.9)
    focal_len = jax.random.uniform(keys[4], (1,), minval=1.9, maxval=2.3)
    return jnp.concatenate([lead, rest, across, depth, focal_len])


def tile_slots(key):
    slot_order = owner_slots(key)
    order = view_tiles(key)
    per_tile = LMAX // N_SPACE
    tiles = order.reshape(VIEWS, N_SPACE, TILE_DEV)
    index = tiles[:, :, :, None] * per_tile + jnp.arange(per_tile, dtype=jnp.int32)
    return slot_order[:, index]


def draw_gaussians(key, part):
    slot_order = owner_slots(key)
    camera = base_camera(key)
    key = jax.random.fold_in(key, 11)
    keys = jax.random.split(key, 10)
    count = GDEV * N_SPACE
    per_tile = LMAX // N_SPACE
    place = jnp.argsort(slot_order, axis=1, stable=True).reshape(count)
    homed = place < TILES_VIEW * per_tile
    region = jnp.minimum(place // per_tile, TILES_VIEW - 1)
    center_u = ((44 + region % 32) * 16 + 8 - 960).astype(jnp.float32) / 540.0
    center_v = ((18 + region // 32) * 16 + 8 - 540).astype(jnp.float32) / 540.0
    jitter = jax.random.uniform(keys[0], (2, count), minval=-8.0 / 540.0, maxval=8.0 / 540.0)
    log_scales = jax.random.uniform(keys[2], (3, count), minval=-5.4, maxval=-3.8)
    harmonics = 0.3 * jax.random.truncated_normal(keys[6], -3.0, 3.0, (48, count))
    share = 0.02
    bright_low = -1.0
    faint_low = -6.0
    wide = jax.random.uniform(keys[1], (2, count), minval=-0.8, maxval=0.8)
    screen_u = jnp.where(homed, center_u + jitter[0], wide[0])
    screen_v = jnp.where(homed, center_v + jitter[1], wide[1])
    depth = 3.6 + 1.8 * (jnp.arange(count, dtype=jnp.int32).astype(jnp.float32) + 0.5) / count
    view_rot = rotation_rows(camera[0:4])
    focal_len = camera[7]
    relative = [screen_u * depth / focal_len - camera[4], screen_v * depth / focal_len - camera[5], depth - camera[6]]
    centers = jnp.stack([sum((view_rot[j][i] * relative[j] for j in range(3))) for i in range(3)])
    quat_lead = jax.random.uniform(keys[3], (1, count), minval=1.0, maxval=2.0)
    quat_rest = jax.random.uniform(keys[4], (3, count), minval=-1.0, maxval=1.0)
    picker = jax.random.uniform(keys[5], (1, count))
    bright = jax.random.uniform(keys[7], (1, count), minval=bright_low, maxval=2.0)
    faint = jax.random.uniform(keys[8], (1, count), minval=faint_low, maxval=-3.5)
    opacity = jnp.where(picker < share, bright, faint)
    return jnp.concatenate([centers, log_scales, quat_lead, quat_rest, opacity, harmonics], axis=0).astype(jnp.float32)


def draw_camera_table(key, part):
    camera = base_camera(key)
    key = jax.random.fold_in(key, 12)
    keys = jax.random.split(key, 5)
    jitter = jnp.concatenate([jax.random.uniform(keys[0], (CAMS, 1), minval=-0.02, maxval=0.02), jax.random.uniform(keys[1], (CAMS, 3), minval=-0.008, maxval=0.008), jax.random.uniform(keys[2], (CAMS, 2), minval=-0.02, maxval=0.02), jax.random.uniform(keys[3], (CAMS, 1), minval=-0.05, maxval=0.05), jax.random.uniform(keys[4], (CAMS, 1), minval=-0.02, maxval=0.02)], axis=1)
    return (camera[None, :] + jitter).astype(jnp.float32)


def draw_tile_plan(key, part):
    order = view_tiles(key)
    key = jax.random.fold_in(key, 13)
    return ((18 + order // 32) * 120 + 44 + order % 32).astype(jnp.int32)


def draw_requests(key, part):
    slots = tile_slots(key)
    sigma = request_order(key)
    key = jax.random.fold_in(key, 14)
    by_place = slots.transpose(1, 2, 0, 3, 4).reshape(VIEWS, N_SPACE, N_SPACE, CAP)
    inverse = jnp.argsort(sigma, axis=3, stable=True)
    return jnp.take_along_axis(by_place, inverse, axis=3).astype(jnp.int32)


def draw_tile_lists(key, part):
    slots = tile_slots(key)
    sigma = request_order(key)
    key = jax.random.fold_in(key, 15)
    per_tile = LMAX // N_SPACE
    slots_tile = slots.transpose(1, 2, 3, 0, 4)
    positions = sigma.reshape(VIEWS, N_SPACE, N_SPACE, TILE_DEV, per_tile).transpose(0, 1, 3, 2, 4)
    owner_ids = jnp.arange(N_SPACE, dtype=jnp.int32)[None, None, None, :, None]
    entries = (owner_ids * CAP + positions).reshape(VIEWS, TILES_VIEW, LMAX)
    depth_keys = (owner_ids * GDEV + slots_tile).reshape(VIEWS, TILES_VIEW, LMAX)
    rank = jnp.argsort(depth_keys, axis=2, stable=True)
    return jnp.take_along_axis(entries, rank, axis=2).astype(jnp.int32)


def draw_tile_lengths(key, part):
    key = jax.random.fold_in(key, 16)
    key_len, key_top = jax.random.split(key, 2)
    lengths = jax.random.randint(key_len, (VIEWS, TILES_VIEW), LMAX // 4, LMAX + 1)
    longest = jax.random.randint(key_top, (VIEWS, 1), 0, TILES_VIEW)
    lengths = jnp.where(jnp.arange(TILES_VIEW, dtype=jnp.int32)[None, :] == longest, LMAX, lengths)
    return lengths.astype(jnp.int32)


def touch_ends(drawn, rng, least, largest):
    spot = [jax.random.randint(jax.random.fold_in(rng, axis), (), 0, length) for axis, length in enumerate(drawn.shape)]
    main_axis = drawn.shape.index(max(drawn.shape))
    neighbour = spot[:main_axis] + [(spot[main_axis] + 1) % drawn.shape[main_axis]] + spot[main_axis + 1:]
    return drawn.at[tuple(spot)].set(least).at[tuple(neighbour)].set(largest)


def shard_levels(own_key, extent, cuts, low, largest):
    level = 1.0
    for dim, parts in cuts:
        heights = jax.random.uniform(jax.random.fold_in(jax.random.fold_in(own_key, 6), dim), (parts,), jnp.float32, low / len(cuts), largest / len(cuts))
        level = level * jnp.repeat(jnp.exp(heights), extent[dim] // parts).reshape((-1,) + (1,) * (len(extent) - 1 - dim))
    return level


def gaussian(own_key, shape, spread, most, shards=(), kind=jnp.bfloat16):
    values = spread * jax.random.normal(own_key, shape, jnp.float32)
    if shards:
        values = values * shard_levels(own_key, shape, shards, -0.22, 0.18)
    return jnp.clip(values, -most, most).astype(kind)


def setup_inputs(seed: int = 0) -> dict:
    seeds = jax.random.split(jax.random.key(seed), 9)
    return {
        "gaussians": draw_gaussians(jax.random.fold_in(seeds[8], 71), 0),
        "camera_table": draw_camera_table(jax.random.fold_in(seeds[8], 71), 0),
        "view_camera": touch_ends(jax.random.randint(seeds[2], (VIEWS,), 0, CAMS), jax.random.fold_in(seeds[2], 1), 0, CAMS - 1).astype(jnp.int32),
        "tile_plan": draw_tile_plan(jax.random.fold_in(seeds[8], 71), 0),
        "requests": draw_requests(jax.random.fold_in(seeds[8], 71), 0),
        "tile_lists": draw_tile_lists(jax.random.fold_in(seeds[8], 71), 0),
        "tile_lengths": draw_tile_lengths(jax.random.fold_in(seeds[8], 71), 0),
        "pixel_grad": gaussian(seeds[7], (VIEWS, TILES_VIEW, 3, PIX), 0.1, 0.625, ((0, 4), (1, 8)), jnp.float32),
    }


sh_zero = 0.28209479177387814
sh_one = 0.4886025119029199
sh_two = (1.0925484305920792, -1.0925484305920792, 0.31539156525252005, -1.0925484305920792, 0.5462742152960396)
sh_three = (-0.5900435899266435, 2.890611442640554, -0.4570457994644658, 0.3731763325901154, -0.4570457994644658, 1.445305721320277, -0.5900435899266435)
dilation = 0.3 / 291600.0
highest = lax.Precision.HIGHEST

def quat_matrix(quat_w, quat_x, quat_y, quat_z):
    length = jnp.sqrt(quat_w * quat_w + quat_x * quat_x + quat_y * quat_y + quat_z * quat_z)
    unit_w = quat_w / length
    unit_x = quat_x / length
    unit_y = quat_y / length
    unit_z = quat_z / length
    return [[1.0 - 2.0 * (unit_y * unit_y + unit_z * unit_z), 2.0 * (unit_x * unit_y - unit_w * unit_z), 2.0 * (unit_x * unit_z + unit_w * unit_y)], [2.0 * (unit_x * unit_y + unit_w * unit_z), 1.0 - 2.0 * (unit_x * unit_x + unit_z * unit_z), 2.0 * (unit_y * unit_z - unit_w * unit_x)], [2.0 * (unit_x * unit_z - unit_w * unit_y), 2.0 * (unit_y * unit_z + unit_w * unit_x), 1.0 - 2.0 * (unit_x * unit_x + unit_y * unit_y)]]

def sh_basis(dir_x, dir_y, dir_z):
    sq_x = dir_x * dir_x
    sq_y = dir_y * dir_y
    sq_z = dir_z * dir_z
    return [sh_zero * jnp.ones_like(dir_x), -sh_one * dir_y, sh_one * dir_z, -sh_one * dir_x, sh_two[0] * dir_x * dir_y, sh_two[1] * dir_y * dir_z, sh_two[2] * (2.0 * sq_z - sq_x - sq_y), sh_two[3] * dir_x * dir_z, sh_two[4] * (sq_x - sq_y), sh_three[0] * dir_y * (3.0 * sq_x - sq_y), sh_three[1] * dir_x * dir_y * dir_z, sh_three[2] * dir_y * (4.0 * sq_z - sq_x - sq_y), sh_three[3] * dir_z * (2.0 * sq_z - 3.0 * sq_x - 3.0 * sq_y), sh_three[4] * dir_x * (4.0 * sq_z - sq_x - sq_y), sh_three[5] * dir_z * (sq_x - sq_y), sh_three[6] * dir_x * (sq_x - 3.0 * sq_y)]

def project(params, camera):
    center = [params[0], params[1], params[2]]
    scales = [jnp.exp(params[3]), jnp.exp(params[4]), jnp.exp(params[5])]
    own_rot = quat_matrix(params[6], params[7], params[8], params[9])
    view_rot = quat_matrix(camera[0], camera[1], camera[2], camera[3])
    offset_cam = [camera[4], camera[5], camera[6]]
    focal_len = camera[7]
    in_camera = [sum((view_rot[i][j] * center[j] for j in range(3))) + offset_cam[i] for i in range(3)]
    shaped = [[own_rot[i][k] * scales[k] for k in range(3)] for i in range(3)]
    turned = [[sum((view_rot[i][j] * shaped[j][k] for j in range(3))) for k in range(3)] for i in range(3)]
    inv_depth = 1.0 / in_camera[2]
    screen_u = focal_len * in_camera[0] * inv_depth
    screen_v = focal_len * in_camera[1] * inv_depth
    jac_u = [focal_len * inv_depth * turned[0][k] - screen_u * inv_depth * turned[2][k] for k in range(3)]
    jac_v = [focal_len * inv_depth * turned[1][k] - screen_v * inv_depth * turned[2][k] for k in range(3)]
    cov_uu = sum((jac_u[k] * jac_u[k] for k in range(3))) + dilation
    cov_uv = sum((jac_u[k] * jac_v[k] for k in range(3)))
    cov_vv = sum((jac_v[k] * jac_v[k] for k in range(3))) + dilation
    determinant = cov_uu * cov_vv - cov_uv * cov_uv
    opacity = jax.nn.sigmoid(params[10])
    eye_pos = [-sum((view_rot[j][i] * offset_cam[j] for j in range(3))) for i in range(3)]
    toward = [center[i] - eye_pos[i] for i in range(3)]
    length = jnp.sqrt(toward[0] * toward[0] + toward[1] * toward[1] + toward[2] * toward[2])
    basis = sh_basis(toward[0] / length, toward[1] / length, toward[2] / length)
    colors = [0.5 + sum((basis[k] * params[11 + 3 * k + h] for k in range(16))) for h in range(3)]
    return jnp.stack([screen_u, screen_v, cov_vv / determinant, -cov_uv / determinant, cov_uu / determinant, opacity] + colors)

def pixel_points(tile_one):
    pixel = jnp.arange(256, dtype=jnp.int32)
    column = tile_one % 120 * 16 + pixel % 16
    row_at = tile_one // 120 * 16 + pixel // 16
    point_u = (column.astype(jnp.float32) + 0.5 - 960.0) / 540.0
    point_v = (row_at.astype(jnp.float32) + 0.5 - 540.0) / 540.0
    return (point_u, point_v)

def render_tiles(features, entries, lengths, tile_ids):

    def one_tile(args):
        entry_row, length_one, tile_one = args
        columns = jnp.take(features, entry_row, axis=1)
        point_u, point_v = pixel_points(tile_one)
        diff_u = point_u[:, None] - columns[0][None, :]
        diff_v = point_v[:, None] - columns[1][None, :]
        power = -0.5 * (columns[2][None, :] * diff_u * diff_u + 2.0 * columns[3][None, :] * diff_u * diff_v + columns[4][None, :] * diff_v * diff_v)
        alpha = columns[5][None, :] * jnp.exp(power)
        alive = jnp.arange(entry_row.shape[0], dtype=jnp.int32) < length_one
        alpha = jnp.where(alive[None, :], alpha, 0.0)
        logs = jnp.log1p(-alpha)
        before = jnp.cumsum(logs, axis=1) - logs
        weights = alpha * jnp.exp(before)
        return lax.dot_general(columns[6:9], weights, (((1,), (1,)), ((), ())), precision=highest)
    return lax.map(one_tile, (entries, lengths, tile_ids))

def reference(gaussians, camera_table, view_camera, tile_plan, requests, tile_lists, tile_lengths, pixel_grad):
    view_ids = jnp.repeat(view_camera, N_SPACE)
    requests_all = requests.reshape(VIEWS * N_SPACE, N_SPACE, CAP)
    plan_all = tile_plan.reshape(VIEWS * N_SPACE, TILE_DEV)
    lists_all = tile_lists.reshape(VIEWS * N_SPACE, TILE_DEV, LMAX)
    lengths_all = tile_lengths.reshape(VIEWS * N_SPACE, TILE_DEV)
    owner_base = (jnp.arange(N_SPACE, dtype=jnp.int32) * GDEV)[:, None]

    def forward(params):

        def one_device(args):
            view_id, requests_dev, plan_dev, lists_dev, lengths_dev = args
            camera = camera_table[view_id]
            picked = jnp.take(params, (requests_dev + owner_base).reshape(-1), axis=1)
            features = project(picked, camera)
            return render_tiles(features, lists_dev, lengths_dev, plan_dev)
        images = lax.map(jax.checkpoint(one_device), (view_ids, requests_all, plan_all, lists_all, lengths_all))
        return images.reshape(VIEWS, TILES_VIEW, 3, PIX)
    rendered, back = jax.vjp(forward, gaussians)
    gaussian_grad, = back(pixel_grad)
    return (rendered, gaussian_grad)
```

```python
import functools
import math

import jax
import jax.numpy as jnp
import numpy as np
from jax import lax
from jax.experimental import pallas as pl
from jax.experimental.pallas import tpu as pltpu
from jax.sharding import PartitionSpec as P

sh_zero = 0.28209479177387814
sh_one = 0.4886025119029199
sh_two = (
    1.0925484305920792,
    -1.0925484305920792,
    0.31539156525252005,
    -1.0925484305920792,
    0.5462742152960396,
)
sh_three = (
    -0.5900435899266435,
    2.890611442640554,
    -0.4570457994644658,
    0.3731763325901154,
    -0.4570457994644658,
    1.445305721320277,
    -0.5900435899266435,
)
dilation = 0.3 / 291600.0
LOG2E = math.log2(math.e)
HALF = 540.0
F32 = jnp.float32
BF16 = jnp.bfloat16
LANES = 128
VMEM = pl.BlockSpec(memory_space=pltpu.VMEM)


def quat_matrix(quat_w, quat_x, quat_y, quat_z):
    inv = 1.0 / jnp.sqrt(quat_w * quat_w + quat_x * quat_x + quat_y * quat_y + quat_z * quat_z)
    w, x, y, z = quat_w * inv, quat_x * inv, quat_y * inv, quat_z * inv
    return [
        [1.0 - 2.0 * (y * y + z * z), 2.0 * (x * y - w * z), 2.0 * (x * z + w * y)],
        [2.0 * (x * y + w * z), 1.0 - 2.0 * (x * x + z * z), 2.0 * (y * z - w * x)],
        [2.0 * (x * z - w * y), 2.0 * (y * z + w * x), 1.0 - 2.0 * (x * x + y * y)],
    ]


def sh_basis(dir_x, dir_y, dir_z):
    sq_x = dir_x * dir_x
    sq_y = dir_y * dir_y
    sq_z = dir_z * dir_z
    return [
        -sh_one * dir_y,
        sh_one * dir_z,
        -sh_one * dir_x,
        sh_two[0] * dir_x * dir_y,
        sh_two[1] * dir_y * dir_z,
        sh_two[2] * (2.0 * sq_z - sq_x - sq_y),
        sh_two[3] * dir_x * dir_z,
        sh_two[4] * (sq_x - sq_y),
        sh_three[0] * dir_y * (3.0 * sq_x - sq_y),
        sh_three[1] * dir_x * dir_y * dir_z,
        sh_three[2] * dir_y * (4.0 * sq_z - sq_x - sq_y),
        sh_three[3] * dir_z * (2.0 * sq_z - 3.0 * sq_x - 3.0 * sq_y),
        sh_three[4] * dir_x * (4.0 * sq_z - sq_x - sq_y),
        sh_three[5] * dir_z * (sq_x - sq_y),
        sh_three[6] * dir_x * (sq_x - 3.0 * sq_y),
    ]


def geometry(params, camera):
    center = params[0:3]
    scales = [jnp.exp(params[3]), jnp.exp(params[4]), jnp.exp(params[5])]
    own_rot = quat_matrix(*params[6:10])
    view_rot, offset_cam, focal_len = camera
    in_camera = [
        sum((view_rot[i][j] * center[j] for j in range(3))) + offset_cam[i] for i in range(3)
    ]
    shaped = [[own_rot[i][k] * scales[k] for k in range(3)] for i in range(3)]
    turned = [
        [sum((view_rot[i][j] * shaped[j][k] for j in range(3))) for k in range(3)] for i in range(3)
    ]
    inv_depth = 1.0 / in_camera[2]
    screen_u = focal_len * in_camera[0] * inv_depth
    screen_v = focal_len * in_camera[1] * inv_depth
    jac_u = [
        focal_len * inv_depth * turned[0][k] - screen_u * inv_depth * turned[2][k] for k in range(3)
    ]
    jac_v = [
        focal_len * inv_depth * turned[1][k] - screen_v * inv_depth * turned[2][k] for k in range(3)
    ]
    cov_uu = sum((jac_u[k] * jac_u[k] for k in range(3))) + dilation
    cov_uv = sum((jac_u[k] * jac_v[k] for k in range(3)))
    cov_vv = sum((jac_v[k] * jac_v[k] for k in range(3))) + dilation
    inv_det = 1.0 / (cov_uu * cov_vv - cov_uv * cov_uv)
    return [screen_u, screen_v, cov_vv * inv_det, -cov_uv * inv_det, cov_uu * inv_det]


def directional(center, camera):
    view_rot, offset_cam, _ = camera
    toward = [
        center[i] + sum((view_rot[j][i] * offset_cam[j] for j in range(3))) for i in range(3)
    ]
    inv = 1.0 / jnp.sqrt(toward[0] * toward[0] + toward[1] * toward[1] + toward[2] * toward[2])
    return sh_basis(toward[0] * inv, toward[1] * inv, toward[2] * inv)


def unpack_camera(rows):
    full = [jnp.broadcast_to(rows[i : i + 1], (8, LANES)) for i in range(8)]
    return (quat_matrix(*full[0:4]), full[4:7], full[7])


def project_kernel(params_ref, camera_ref, out_ref):
    camera = unpack_camera(camera_ref[...])
    params = [params_ref[i] for i in range(11)]
    feats = geometry(params, camera)
    logit = params[10]
    feats.append(jnp.minimum(logit, 0.0) - jnp.log1p(jnp.exp(-jnp.abs(logit))))
    basis = directional(params[0:3], camera)
    for h in range(3):
        total = 0.5 + sh_zero * params_ref[11 + h]
        for k in range(1, 16):
            total = total + basis[k - 1] * params_ref[11 + 3 * k + h]
        feats.append(total)
    for i in range(9):
        out_ref[i] = feats[i]


def project_all(params, camera):
    blocks = params.shape[1] // 8
    return pl.pallas_call(
        project_kernel,
        grid=(blocks,),
        in_specs=[
            pl.BlockSpec((params.shape[0], 8, LANES), lambda i: (0, i, 0)),
            pl.BlockSpec((8, LANES), lambda i: (0, 0)),
        ],
        out_specs=pl.BlockSpec((9, 8, LANES), lambda i: (0, i, 0)),
        out_shape=jax.ShapeDtypeStruct((9,) + params.shape[1:], F32),
        name="project",
    )(params, camera)


def lane_pick(rows, lanes):
    return jnp.take_along_axis(rows, lanes, axis=1, mode="promise_in_bounds")


def order_kernel(reps, request_ref, place_ref, out_ref):
    groups = request_ref.shape[0]
    place = place_ref[...].reshape(groups * reps, LANES)
    lanes = place & (LANES - 1)
    high = place >> 7
    result = jnp.zeros_like(place)
    for r in range(reps):
        table = jnp.broadcast_to(request_ref[:, r : r + 1, :], (groups, reps, LANES))
        picked = lane_pick(table.reshape(groups * reps, LANES), lanes)
        result = jnp.where(high == r, picked, result)
    out_ref[...] = result.reshape(groups, reps, LANES)


def invert_kernel(index_ref, out_ref):
    rows = index_ref.shape[0]
    high_iota = lax.broadcasted_iota(jnp.int32, (rows, 8 * LANES), 0)
    lane_iota = lax.broadcasted_iota(jnp.int32, (LANES, 8 * LANES), 0)
    column = lax.broadcasted_iota(jnp.int32, (1, 8 * LANES), 1)
    total = jnp.zeros((2 * rows, LANES), F32)
    for m in range(rows // 8):
        block = index_ref[8 * m : 8 * m + 8, :]
        flat = jnp.concatenate([block[s : s + 1] for s in range(8)], axis=1)
        hit = high_iota == (flat >> 7)
        row_value = (column // LANES + 8 * m).astype(F32)
        lane_value = (column % LANES).astype(F32)
        left = jnp.concatenate(
            [jnp.where(hit, row_value, 0.0), jnp.where(hit, lane_value, 0.0)], axis=0
        ).astype(BF16)
        right = jnp.where(lane_iota == (flat & (LANES - 1)), 1.0, 0.0).astype(BF16)
        total = total + lax.dot_general(
            left, right, (((1,), (1,)), ((), ())), preferred_element_type=F32
        )
    out_ref[...] = (total[:rows] * float(LANES) + total[rows:]).astype(jnp.int32)


def pick_block(load_row, index, source_rows):
    lanes = index & (LANES - 1)
    high = index >> 7

    def step(r, totals):
        hit = high == r
        return tuple(
            jnp.where(hit, lane_pick(jnp.broadcast_to(load_row(f, r), (8, LANES)), lanes), totals[f])
            for f in range(9)
        )

    start = tuple(jnp.zeros((8, LANES), F32) for _ in range(9))
    return lax.fori_loop(0, source_rows, step, start, unroll=8)


def gather_kernel(feature_ref, index_ref, out_ref):
    rows = feature_ref.shape[1]

    def block(m, carry):
        index = index_ref[pl.ds(pl.multiple_of(8 * m, 8), 8), :]
        picked = pick_block(lambda f, r: feature_ref[f, pl.ds(r, 1), :], index, rows)
        for f in range(9):
            out_ref[m, f] = picked[f]
        return carry

    lax.fori_loop(0, index_ref.shape[0] // 8, block, 0)


def ungather_kernel(grad_ref, index_ref, camera_ref, out_ref):
    rows = index_ref.shape[0]
    blocks = rows // 8

    def block(m, carry):
        index = index_ref[pl.ds(pl.multiple_of(8 * m, 8), 8), :]
        picked = pick_block(
            lambda f, r: grad_ref[r // 8, f, pl.ds(r % 8, 1), :], index, rows
        )
        for f in range(9):
            out_ref[f * blocks + m] = picked[f]
        return carry

    lax.fori_loop(0, blocks, block, 0)
    out_ref[9 * blocks] = camera_ref[...]


def backproject_kernel(views, blocks, params_ref, grad_ref, out_ref):
    m = pl.program_id(0)
    params = [params_ref[i] for i in range(11)]
    kept = [None] * 11
    for v in range(views):
        camera = unpack_camera(grad_ref[v, 9 * blocks])
        grads = [grad_ref[v, f * blocks + m] for f in range(9)]
        _, back = jax.vjp(lambda *p: geometry(list(p), camera), *params[0:10])
        shares = list(back(grads[0:5]))
        basis, back_dir = jax.vjp(lambda *c: directional(list(c), camera), *params[0:3])
        basis_grads = []
        for k in range(16):
            value = 0.0
            for h in range(3):
                at = 11 + 3 * k + h
                scale = sh_zero if k == 0 else basis[k - 1]
                share = scale * grads[6 + h]
                out_ref[at] = share if v == 0 else out_ref[at] + share
                if k:
                    value = value + params_ref[at] * grads[6 + h]
            if k:
                basis_grads.append(value)
        center_shares = back_dir(basis_grads)
        for i in range(3):
            shares[i] = shares[i] + center_shares[i]
        shares.append(grads[5] * jax.nn.sigmoid(-params[10]))
        kept = [s if t is None else t + s for s, t in zip(shares, kept)]
    for i in range(11):
        out_ref[i] = kept[i]


def backproject(params, grads):
    views, total = grads.shape[0], grads.shape[1]
    blocks = params.shape[1] // 8
    spec = pl.BlockSpec((params.shape[0], 8, LANES), lambda i: (0, i, 0))
    return pl.pallas_call(
        functools.partial(backproject_kernel, views, blocks),
        grid=(blocks,),
        in_specs=[
            spec,
            pl.BlockSpec((views, total, 8, LANES), lambda i: (0, 0, 0, 0)),
        ],
        out_specs=spec,
        out_shape=jax.ShapeDtypeStruct(params.shape, F32),
        name="backproject",
    )(params, grads)


def split_two(value):
    high = value.astype(BF16)
    return high, (value - high.astype(F32)).astype(BF16)


def split_three(value):
    high = value.astype(BF16).astype(F32)
    rest = value - high
    middle = rest.astype(BF16).astype(F32)
    return high, middle, rest - middle


def pixel_basis():
    pixel = np.arange(256)
    x = (pixel % 16) - 7.5
    y = (pixel // 16) - 7.5
    return np.stack([np.ones(256), x, y, x * x, x * y, y * y])


def spread_matrix():
    basis = pixel_basis()
    matrix = np.zeros((32, 640), np.float32)
    for s in range(3):
        matrix[9 * s : 9 * s + 6, :256] = basis
        for h in range(3):
            matrix[9 * s + 6 + h, 256 + 128 * h : 384 + 128 * h] = 1.0
    return jnp.asarray(matrix, BF16)


def moment_matrix():
    matrix = np.zeros((256, LANES), np.float32)
    matrix[:, 96:102] = pixel_basis().T
    return jnp.asarray(matrix, BF16)


def local_conic(feature_ref, m, center_u, center_v):
    shift_u = (feature_ref[m, 0] - center_u) * HALF
    shift_v = (feature_ref[m, 1] - center_v) * HALF
    scale = 1.0 / (HALF * HALF)
    return shift_u, shift_v, [feature_ref[m, 2 + i] * scale for i in range(3)]


def composite_kernel(
    feature_ref,
    meta_ref,
    pixel_grad_ref,
    spread_ref,
    moment_ref,
    image_ref,
    out_ref,
    coef_ref,
    alpha_ref,
    color_ref,
    weight_ref,
    shade_ref,
    reduce_ref,
    stage_a,
    stage_b,
    sums_ref,
    moments_ref,
):
    blocks = feature_ref.shape[0]
    rows = 8 * blocks
    center_u = meta_ref[0:1, :]
    center_v = meta_ref[1:2, :]
    lengths = meta_ref[2:3, :]
    lane = lax.broadcasted_iota(jnp.int32, (8, LANES), 1)
    sub = lax.broadcasted_iota(jnp.int32, (8, LANES), 0)

    for m in range(blocks):
        su, sv, (ca, cb, cc) = local_conic(feature_ref, m, center_u, center_v)
        place = ((8 * m + sub) * 8 + lane // 16).astype(F32)
        alive = place < lengths
        lin_u = ca * su + cb * sv
        lin_v = cb * su + cc * sv
        const = feature_ref[m, 5] - 0.5 * (lin_u * su + lin_v * sv)
        coefs = [const, lin_u, lin_v, -0.5 * ca, -cb, -0.5 * cc]
        dead = [-1.0e30, 0.0, 0.0, 0.0, 0.0, 0.0]
        coefs = [jnp.where(alive, c * LOG2E, d) for c, d in zip(coefs, dead)]
        coefs += [feature_ref[m, 6 + h] for h in range(3)]
        for i in range(9):
            for s, part in enumerate(split_three(coefs[i])):
                coef_ref[8 * m : 8 * m + 8, 9 * s + i, :] = part
        for i in range(27, 32):
            coef_ref[8 * m : 8 * m + 8, i, :] = jnp.zeros((8, LANES), F32)

    grads = pixel_grad_ref[...]
    high = grads.astype(BF16).astype(F32)
    stacked = jnp.concatenate([high, grads - high, jnp.zeros((32, 256), F32)], axis=0)
    by_pixel = jnp.transpose(stacked).astype(BF16)
    reduce_ref[0:256, :] = by_pixel
    reduce_ref[256:512, :] = by_pixel
    reduce_ref[512:768, :] = moment_ref[...]
    reduce_ref[768:1024, :] = moment_ref[...]

    def expand(i, carry):
        left = jnp.concatenate(
            [jnp.transpose(coef_ref[4 * i + s]) for s in range(4)], axis=0
        ).astype(BF16)
        spread = jnp.dot(left, spread_ref[...], preferred_element_type=F32)
        at = pl.ds(pl.multiple_of(512 * i, 512), 512)
        alpha_ref[at, :] = spread[:, 0:256]
        color_ref[at, :] = spread[:, 256:640]
        return carry

    lax.fori_loop(0, rows // 4, expand, 0)

    parts = [(g, b) for g in range(2) for b in range(2)]
    pixel_grads = {
        (g, b, h): pixel_grad_ref[16 * h + 8 * g : 16 * h + 8 * g + 8, 128 * b : 128 * b + 128]
        for g, b in parts
        for h in range(3)
    }

    def forward(q, carry):
        left, totals = list(carry[0]), list(carry[1])
        for kk in range(8):
            for g in range(2):
                at = pl.ds(pl.multiple_of(128 * q + 16 * kk + 8 * g, 8), 8)
                colors = [color_ref[at, 128 * h : 128 * h + 128] for h in range(3)]
                for b in range(2):
                    n = 2 * g + b
                    cols = slice(128 * b, 128 * b + 128)
                    alpha = jnp.exp2(alpha_ref[at, cols])
                    weight = alpha * left[n]
                    left[n] = left[n] - weight
                    shade = colors[0] * pixel_grads[g, b, 0]
                    shade = shade + colors[1] * pixel_grads[g, b, 1]
                    shade = shade + colors[2] * pixel_grads[g, b, 2]
                    for h in range(3):
                        totals[3 * n + h] = totals[3 * n + h] + weight * colors[h]
                    alpha_ref[at, cols] = alpha
                    weight_ref[at, cols] = weight
                    shade_ref[at, cols] = shade
        return tuple(left), tuple(totals)

    one = jnp.ones((8, LANES), F32)
    zero = jnp.zeros((8, LANES), F32)
    _, totals = lax.fori_loop(0, rows, forward, ((one,) * 4, (zero,) * 12))
    for n, (g, b) in enumerate(parts):
        for h in range(3):
            image_ref[8 * g : 8 * g + 8, h, 128 * b : 128 * b + 128] = totals[3 * n + h]

    def sweep(q, behind, stage):
        behind = list(behind)
        for kk in reversed(range(8)):
            for b in range(2):
                cols = slice(128 * b, 128 * b + 128)
                weights, slopes = [], []
                for g in range(2):
                    n = 2 * g + b
                    at = pl.ds(pl.multiple_of(128 * q + 16 * kk + 8 * g, 8), 8)
                    weight = weight_ref[at, cols]
                    gap = shade_ref[at, cols] - behind[n]
                    weights.append(weight)
                    slopes.append(weight * gap)
                    behind[n] = behind[n] + alpha_ref[at, cols] * gap
                split = split_two(jnp.concatenate(weights, axis=0))
                split += split_two(jnp.concatenate(slopes, axis=0))
                for i in range(4):
                    stage[16 * kk : 16 * kk + 16, 256 * i + 128 * b : 256 * i + 128 * b + 128] = split[i]
        return tuple(behind)

    def reduce_stage(q, stage):
        at = pl.ds(pl.multiple_of(128 * q, 128), 128)
        sums_ref[at, :] = jnp.dot(stage[...], reduce_ref[...], preferred_element_type=F32)

    stage_b[...] = jnp.zeros_like(stage_b)

    def backward(i, behind):
        q = rows - 1 - 2 * i
        reduce_stage(q + 1, stage_b)
        behind = sweep(q, behind, stage_a)
        reduce_stage(q, stage_a)
        return sweep(q - 1, behind, stage_b)

    lax.fori_loop(0, rows // 2, backward, (zero,) * 4)
    reduce_stage(0, stage_b)

    own = lax.broadcasted_iota(jnp.int32, (16, LANES), 0) == (
        lax.broadcasted_iota(jnp.int32, (16, LANES), 1) % 16
    )

    def collect(m, carry):
        for s in range(8):
            q = 8 * m + s
            at = pl.ds(pl.multiple_of(128 * q, 128), 128)
            turned = jnp.transpose(sums_ref[at, :])
            for i in range(6):
                moments_ref[i, s : s + 1, :] = turned[96 + i : 97 + i]
            for h in range(3):
                both = turned[16 * h : 16 * h + 16] + turned[48 + 16 * h : 64 + 16 * h]
                moments_ref[6 + h, s : s + 1, :] = jnp.sum(
                    jnp.where(own, both, 0.0), axis=0, keepdims=True
                )
        su, sv, (ca, cb, cc) = local_conic(feature_ref, m, center_u, center_v)
        m0, mx, my, mxx, mxy, myy = [moments_ref[i] for i in range(6)]
        scale = 1.0 / (HALF * HALF)
        dev_u = mx - su * m0
        dev_v = my - sv * m0
        out_ref[m, 0] = HALF * (ca * dev_u + cb * dev_v)
        out_ref[m, 1] = HALF * (cb * dev_u + cc * dev_v)
        out_ref[m, 2] = -0.5 * scale * (mxx - su * (mx + dev_u))
        out_ref[m, 3] = -scale * (mxy - su * my - sv * dev_u)
        out_ref[m, 4] = -0.5 * scale * (myy - sv * (my + dev_v))
        out_ref[m, 5] = m0
        for h in range(3):
            out_ref[m, 6 + h] = moments_ref[6 + h]
        return carry

    lax.fori_loop(0, blocks, collect, 0)


def composite(features, meta, pixel_grad, tiles):
    blocks = features.shape[0]
    count = blocks * 8 * LANES
    return pl.pallas_call(
        composite_kernel,
        in_specs=[VMEM] * 5,
        out_specs=[VMEM] * 2,
        out_shape=[
            jax.ShapeDtypeStruct((tiles, 3, 256), F32),
            jax.ShapeDtypeStruct((blocks, 9, 8, LANES), F32),
        ],
        scratch_shapes=[
            pltpu.VMEM((8 * blocks, 32, LANES), F32),
            pltpu.VMEM((count, 256), F32),
            pltpu.VMEM((count, 384), F32),
            pltpu.VMEM((count, 256), F32),
            pltpu.VMEM((count, 256), F32),
            pltpu.VMEM((1024, LANES), BF16),
            pltpu.VMEM((128, 1024), BF16),
            pltpu.VMEM((128, 1024), BF16),
            pltpu.VMEM((count + 128, LANES), F32),
            pltpu.VMEM((9, 8, LANES), F32),
        ],
        compiler_params=pltpu.CompilerParams(vmem_limit_bytes=56 * 1024 * 1024),
        name="composite",
    )(features, meta, pixel_grad, spread_matrix(), moment_matrix())


def to_blocks(sent):
    groups, width, reps, _ = sent.shape
    if reps == 8:
        return sent
    rows = sent.transpose(0, 2, 1, 3).reshape(groups * reps // 8, 8, width, LANES)
    return rows.transpose(0, 2, 1, 3)


def from_blocks(blocked, groups, reps):
    if reps == 8:
        return blocked
    width = blocked.shape[1]
    rows = blocked.transpose(0, 2, 1, 3).reshape(groups, reps, width, LANES)
    return rows.transpose(0, 2, 1, 3)


def simple_call(kernel, shape, dtype, name, *args):
    return pl.pallas_call(
        kernel,
        in_specs=[VMEM] * len(args),
        out_specs=VMEM,
        out_shape=jax.ShapeDtypeStruct(shape, dtype),
        name=name,
    )(*args)


def exchange(sent):
    return lax.all_to_all(sent, "space", split_axis=0, concat_axis=0, tiled=True)


def per_device(
    gaussians, camera_table, view_camera, tile_plan, requests, tile_lists, tile_lengths, pixel_grad
):
    groups, cap = requests.shape[2:]
    reps = cap // LANES
    tiles, span = tile_lists.shape[1:]
    slots = gaussians.shape[1]
    rows = slots // LANES
    blocks = rows // 8

    base = jnp.arange(groups, dtype=jnp.int32)[:, None] * cap
    place = tile_lists[0].T.reshape(groups, cap) - base
    wanted = simple_call(
        functools.partial(order_kernel, reps),
        (groups, reps, LANES),
        jnp.int32,
        "order",
        requests[0, 0].reshape(groups, reps, LANES),
        place.reshape(groups, reps, LANES),
    )
    incoming = exchange(wanted).reshape(groups * reps, LANES)

    chosen = (jnp.arange(camera_table.shape[0], dtype=jnp.int32) == view_camera[0]).astype(F32)
    camera = jnp.sum(camera_table * chosen[:, None], axis=0)
    camera = jnp.broadcast_to(camera[:, None], (8, LANES))
    params = gaussians.reshape(gaussians.shape[0], rows, LANES)
    features = project_all(params, camera)

    sent = simple_call(
        gather_kernel, (groups * reps // 8, 9, 8, LANES), F32, "gather", features, incoming
    )
    arrived = to_blocks(exchange(from_blocks(sent, groups, reps)))
    inverse = simple_call(invert_kernel, (rows, LANES), jnp.int32, "invert", incoming)

    plan = tile_plan[0]
    center_u = ((plan % 120 * 16 + 8).astype(F32) - 960.0) / HALF
    center_v = ((plan // 120 * 16 + 8).astype(F32) - 540.0) / HALF
    meta = jnp.stack([center_u, center_v, tile_lengths[0].astype(F32)])
    meta = jnp.tile(meta, (1, LANES // tiles))
    by_color = pixel_grad[0].transpose(1, 0, 2).reshape(3 * tiles, 256)
    image, row_grads = composite(arrived, meta, by_color, tiles)

    returned = to_blocks(exchange(from_blocks(row_grads, groups, reps)))
    packed = simple_call(
        ungather_kernel, (9 * blocks + 1, 8, LANES), F32, "ungather", returned, inverse, camera
    )
    every = lax.all_gather(packed, "view")
    total = backproject(params, every)
    return (image[None], total.reshape(gaussians.shape))


def solution(mesh):
    placed = (
        P(None, "space"),
        P(),
        P("view"),
        P("view", "space"),
        P("view", "space", None, None),
        P("view", "space", None),
        P("view", "space"),
        P("view", "space", None, None),
    )
    return jax.shard_map(
        per_device,
        mesh=mesh,
        in_specs=placed,
        out_specs=(P("view", "space", None, None), P(None, "space")),
        check_vma=False,
    )
```

```python
import functools
import math

import jax
import jax.numpy as jnp
import numpy as np
from jax import lax
from jax.experimental import pallas as pl
from jax.experimental.pallas import tpu as pltpu
from jax.sharding import PartitionSpec as P

sh_zero = 0.28209479177387814
sh_one = 0.4886025119029199
sh_two = (
    1.0925484305920792,
    -1.0925484305920792,
    0.31539156525252005,
    -1.0925484305920792,
    0.5462742152960396,
)
sh_three = (
    -0.5900435899266435,
    2.890611442640554,
    -0.4570457994644658,
    0.3731763325901154,
    -0.4570457994644658,
    1.445305721320277,
    -0.5900435899266435,
)
dilation = 0.3 / 291600.0
LOG2E = math.log2(math.e)
HALF = 540.0
F32 = jnp.float32
BF16 = jnp.bfloat16
LANES = 128
VMEM = pl.BlockSpec(memory_space=pltpu.VMEM)


def quat_matrix(quat_w, quat_x, quat_y, quat_z):
    inv = 1.0 / jnp.sqrt(quat_w * quat_w + quat_x * quat_x + quat_y * quat_y + quat_z * quat_z)
    w, x, y, z = quat_w * inv, quat_x * inv, quat_y * inv, quat_z * inv
    return [
        [1.0 - 2.0 * (y * y + z * z), 2.0 * (x * y - w * z), 2.0 * (x * z + w * y)],
        [2.0 * (x * y + w * z), 1.0 - 2.0 * (x * x + z * z), 2.0 * (y * z - w * x)],
        [2.0 * (x * z - w * y), 2.0 * (y * z + w * x), 1.0 - 2.0 * (x * x + y * y)],
    ]


def sh_basis(dir_x, dir_y, dir_z):
    sq_x = dir_x * dir_x
    sq_y = dir_y * dir_y
    sq_z = dir_z * dir_z
    return [
        -sh_one * dir_y,
        sh_one * dir_z,
        -sh_one * dir_x,
        sh_two[0] * dir_x * dir_y,
        sh_two[1] * dir_y * dir_z,
        sh_two[2] * (2.0 * sq_z - sq_x - sq_y),
        sh_two[3] * dir_x * dir_z,
        sh_two[4] * (sq_x - sq_y),
        sh_three[0] * dir_y * (3.0 * sq_x - sq_y),
        sh_three[1] * dir_x * dir_y * dir_z,
        sh_three[2] * dir_y * (4.0 * sq_z - sq_x - sq_y),
        sh_three[3] * dir_z * (2.0 * sq_z - 3.0 * sq_x - 3.0 * sq_y),
        sh_three[4] * dir_x * (4.0 * sq_z - sq_x - sq_y),
        sh_three[5] * dir_z * (sq_x - sq_y),
        sh_three[6] * dir_x * (sq_x - 3.0 * sq_y),
    ]


def geometry(params, camera):
    center = params[0:3]
    scales = [jnp.exp(params[3]), jnp.exp(params[4]), jnp.exp(params[5])]
    own_rot = quat_matrix(*params[6:10])
    view_rot, offset_cam, focal_len = camera
    in_camera = [
        sum((view_rot[i][j] * center[j] for j in range(3))) + offset_cam[i] for i in range(3)
    ]
    shaped = [[own_rot[i][k] * scales[k] for k in range(3)] for i in range(3)]
    turned = [
        [sum((view_rot[i][j] * shaped[j][k] for j in range(3))) for k in range(3)] for i in range(3)
    ]
    inv_depth = 1.0 / in_camera[2]
    screen_u = focal_len * in_camera[0] * inv_depth
    screen_v = focal_len * in_camera[1] * inv_depth
    jac_u = [
        focal_len * inv_depth * turned[0][k] - screen_u * inv_depth * turned[2][k] for k in range(3)
    ]
    jac_v = [
        focal_len * inv_depth * turned[1][k] - screen_v * inv_depth * turned[2][k] for k in range(3)
    ]
    cov_uu = sum((jac_u[k] * jac_u[k] for k in range(3))) + dilation
    cov_uv = sum((jac_u[k] * jac_v[k] for k in range(3)))
    cov_vv = sum((jac_v[k] * jac_v[k] for k in range(3))) + dilation
    inv_det = 1.0 / (cov_uu * cov_vv - cov_uv * cov_uv)
    return [screen_u, screen_v, cov_vv * inv_det, -cov_uv * inv_det, cov_uu * inv_det]


def directional(center, camera):
    view_rot, offset_cam, _ = camera
    toward = [
        center[i] + sum((view_rot[j][i] * offset_cam[j] for j in range(3))) for i in range(3)
    ]
    inv = 1.0 / jnp.sqrt(toward[0] * toward[0] + toward[1] * toward[1] + toward[2] * toward[2])
    return sh_basis(toward[0] * inv, toward[1] * inv, toward[2] * inv)


def unpack_camera(rows):
    full = [jnp.broadcast_to(rows[i : i + 1], (8, LANES)) for i in range(8)]
    return (quat_matrix(*full[0:4]), full[4:7], full[7])


def project_block(load, camera):
    params = [load(i) for i in range(11)]
    feats = geometry(params, camera)
    logit = params[10]
    feats.append(jnp.minimum(logit, 0.0) - jnp.log1p(jnp.exp(-jnp.abs(logit))))
    basis = directional(params[0:3], camera)
    for h in range(3):
        total = 0.5 + sh_zero * load(11 + h)
        for k in range(1, 16):
            total = total + basis[k - 1] * load(11 + 3 * k + h)
        feats.append(total)
    return feats


def project_kernel(params_ref, camera_ref, out_ref):
    feats = project_block(lambda i: params_ref[i], unpack_camera(camera_ref[...]))
    for i in range(9):
        out_ref[i] = feats[i]


def project_all(params, camera):
    blocks = params.shape[1] // 8
    return pl.pallas_call(
        project_kernel,
        grid=(blocks,),
        in_specs=[
            pl.BlockSpec((params.shape[0], 8, LANES), lambda i: (0, i, 0)),
            pl.BlockSpec((8, LANES), lambda i: (0, 0)),
        ],
        out_specs=pl.BlockSpec((9, 8, LANES), lambda i: (0, i, 0)),
        out_shape=jax.ShapeDtypeStruct((9,) + params.shape[1:], F32),
        name="project",
    )(params, camera)


def lane_pick(rows, lanes):
    return jnp.take_along_axis(rows, lanes, axis=1, mode="promise_in_bounds")


def order_rows(requests, place):
    groups, reps = place.shape[:2]
    place = place.reshape(groups * reps, LANES)
    lanes = place & (LANES - 1)
    high = place >> 7
    result = jnp.zeros_like(place)
    for r in range(reps):
        table = jnp.broadcast_to(requests[:, r : r + 1, :], (groups, reps, LANES))
        picked = lane_pick(table.reshape(groups * reps, LANES), lanes)
        result = jnp.where(high == r, picked, result)
    return result.reshape(groups, reps, LANES)


def order_kernel(request_ref, place_ref, out_ref):
    out_ref[...] = order_rows(request_ref[...], place_ref[...])


def invert_rows(blocks):
    rows = 8 * len(blocks)
    high_iota = lax.broadcasted_iota(jnp.int32, (rows, 8 * LANES), 0)
    lane_iota = lax.broadcasted_iota(jnp.int32, (LANES, 8 * LANES), 0)
    column = lax.broadcasted_iota(jnp.int32, (1, 8 * LANES), 1)
    total = jnp.zeros((2 * rows, LANES), F32)
    for m, block in enumerate(blocks):
        flat = jnp.concatenate([block[s : s + 1] for s in range(8)], axis=1)
        hit = high_iota == (flat >> 7)
        row_value = ((column >> 7) + 8 * m).astype(F32)
        lane_value = (column & (LANES - 1)).astype(F32)
        left = jnp.concatenate(
            [jnp.where(hit, row_value, 0.0), jnp.where(hit, lane_value, 0.0)], axis=0
        ).astype(BF16)
        right = jnp.where(lane_iota == (flat & (LANES - 1)), 1.0, 0.0).astype(BF16)
        total = total + lax.dot_general(
            left, right, (((1,), (1,)), ((), ())), preferred_element_type=F32
        )
    return (total[:rows] * float(LANES) + total[rows:]).astype(jnp.int32)


def invert_kernel(index_ref, out_ref):
    rows = index_ref.shape[0]
    out_ref[...] = invert_rows([index_ref[8 * m : 8 * m + 8, :] for m in range(rows // 8)])


def pick_block(load_row, index, source_rows):
    lanes = index & (LANES - 1)
    high = index >> 7

    def step(r, totals):
        hit = high == r
        return tuple(
            jnp.where(hit, lane_pick(jnp.broadcast_to(load_row(f, r), (8, LANES)), lanes), totals[f])
            for f in range(9)
        )

    start = tuple(jnp.zeros((8, LANES), F32) for _ in range(9))
    return lax.fori_loop(0, source_rows, step, start, unroll=8)


def gather_kernel(feature_ref, index_ref, out_ref):
    rows = feature_ref.shape[1]

    def block(m, carry):
        index = index_ref[pl.ds(pl.multiple_of(8 * m, 8), 8), :]
        picked = pick_block(lambda f, r: feature_ref[f, pl.ds(r, 1), :], index, rows)
        for f in range(9):
            out_ref[m, f] = picked[f]
        return carry

    lax.fori_loop(0, index_ref.shape[0] // 8, block, 0)


def ungather_kernel(grad_ref, index_ref, camera_ref, out_ref):
    rows = index_ref.shape[0]
    blocks = rows // 8

    def block(m, carry):
        index = index_ref[pl.ds(pl.multiple_of(8 * m, 8), 8), :]
        picked = pick_block(
            lambda f, r: grad_ref[r // 8, f, pl.ds(r % 8, 1), :], index, rows
        )
        for f in range(9):
            out_ref[f * blocks + m] = picked[f]
        return carry

    lax.fori_loop(0, blocks, block, 0)
    out_ref[9 * blocks] = camera_ref[...]


def backproject_block(load, cameras, grads, load_out, store_out):
    params = [load(i) for i in range(11)]
    kept = [None] * 11
    for v, camera in enumerate(cameras):
        _, back = jax.vjp(lambda *p: geometry(list(p), camera), *params[0:10])
        shares = list(back(grads[v][0:5]))
        basis, back_dir = jax.vjp(lambda *c: directional(list(c), camera), *params[0:3])
        basis_grads = []
        for k in range(16):
            value = 0.0
            for h in range(3):
                at = 11 + 3 * k + h
                scale = sh_zero if k == 0 else basis[k - 1]
                share = scale * grads[v][6 + h]
                store_out(at, share if v == 0 else load_out(at) + share)
                if k:
                    value = value + load(at) * grads[v][6 + h]
            if k:
                basis_grads.append(value)
        center_shares = back_dir(basis_grads)
        for i in range(3):
            shares[i] = shares[i] + center_shares[i]
        shares.append(grads[v][5] * jax.nn.sigmoid(-params[10]))
        kept = [s if t is None else t + s for s, t in zip(shares, kept)]
    for i in range(11):
        store_out(i, kept[i])


def backproject_kernel(views, blocks, params_ref, grad_ref, out_ref):
    m = pl.program_id(0)

    def store(i, value):
        out_ref[i] = value

    backproject_block(
        lambda i: params_ref[i],
        [unpack_camera(grad_ref[v, 9 * blocks]) for v in range(views)],
        [[grad_ref[v, f * blocks + m] for f in range(9)] for v in range(views)],
        lambda i: out_ref[i],
        store,
    )


def remote(src, dst, send, recv, device):
    return pltpu.make_async_remote_copy(
        src_ref=src,
        dst_ref=dst,
        send_sem=send,
        recv_sem=recv,
        device_id=device,
        device_id_type=pl.DeviceIdType.MESH,
    )


def request_kernel(
    groups,
    request_ref,
    place_ref,
    params_ref,
    camera_ref,
    arrived_ref,
    inverse_ref,
    wanted,
    incoming,
    features,
    outbox,
    ask_send,
    ask_recv,
    row_send,
    row_recv,
):
    me = lax.axis_index("space")
    view = lax.axis_index("view")
    rows = features.shape[1]

    def peer(d):
        return lax.rem(me + (d + groups), groups)

    barrier = pltpu.get_barrier_semaphore()
    for d in range(1, groups):
        pl.semaphore_signal(
            barrier, inc=1, device_id=(peer(d), view), device_id_type=pl.DeviceIdType.MESH
        )
    wanted[...] = order_rows(request_ref[...], place_ref[...])
    pl.semaphore_wait(barrier, groups - 1)

    asks = []
    for d in range(1, groups):
        to = peer(d)
        ask = remote(
            wanted.at[to], incoming.at[me], ask_send.at[d], ask_recv.at[d], (to, view)
        )
        ask.start()
        asks.append(ask)
    incoming[me] = wanted[me]

    camera = unpack_camera(camera_ref[...])

    def project(m, carry):
        at = pl.ds(pl.multiple_of(8 * m, 8), 8)
        feats = project_block(lambda i: params_ref[i, at, :], camera)
        for i in range(9):
            features[i, at, :] = feats[i]
        return carry

    lax.fori_loop(0, rows // 8, project, 0)

    answers = []
    for d in range(groups):
        if d:
            asks[d - 1].wait_recv()
        to = peer(-d)
        picked = pick_block(lambda f, r: features[f, pl.ds(r, 1), :], incoming[to], rows)
        box = outbox.at[d] if d else arrived_ref.at[me]
        for f in range(9):
            box[f] = picked[f]
        if d:
            answer = remote(
                outbox.at[d], arrived_ref.at[me], row_send.at[d], row_recv.at[d], (to, view)
            )
            answer.start()
            answers.append(answer)
    inverse_ref[...] = invert_rows([incoming[s] for s in range(groups)])
    for ask in asks:
        ask.wait_send()
    for answer in answers:
        answer.wait()


def request_rows(requests, place, params, camera):
    groups = requests.shape[0]
    rows = params.shape[1]
    return pl.pallas_call(
        functools.partial(request_kernel, groups),
        in_specs=[VMEM] * 4,
        out_specs=[VMEM] * 2,
        out_shape=[
            jax.ShapeDtypeStruct((groups, 9, 8, LANES), F32),
            jax.ShapeDtypeStruct((rows, LANES), jnp.int32),
        ],
        scratch_shapes=[
            pltpu.VMEM((groups, 8, LANES), jnp.int32),
            pltpu.VMEM((groups, 8, LANES), jnp.int32),
            pltpu.VMEM((9, rows, LANES), F32),
            pltpu.VMEM((groups, 9, 8, LANES), F32),
        ]
        + [pltpu.SemaphoreType.DMA((groups,))] * 4,
        compiler_params=pltpu.CompilerParams(
            collective_id=0, has_side_effects=True, vmem_limit_bytes=32 * 1024 * 1024
        ),
        name="request",
    )(requests, place, params, camera)


def return_kernel(
    groups,
    grad_ref,
    index_ref,
    camera_ref,
    params_ref,
    out_ref,
    landed,
    every,
    cameras,
    row_send,
    row_recv,
    cam_send,
    cam_recv,
    view_send,
    view_recv,
):
    me = lax.axis_index("space")
    view = lax.axis_index("view")
    core = lax.rem(view, 2)
    beside = view + 1 - 2 * core
    across = lax.rem(view + 2, 4)
    diagonal = lax.rem(beside + 2, 4)
    rows = index_ref.shape[0]
    blocks = rows // 8

    def peer(d):
        return lax.rem(me + (d + groups), groups)

    barrier = pltpu.get_barrier_semaphore()
    for device in [(peer(d), view) for d in range(1, groups)] + [
        (me, v) for v in (beside, across, diagonal)
    ]:
        pl.semaphore_signal(
            barrier, inc=1, device_id=device, device_id_type=pl.DeviceIdType.MESH
        )
    pl.semaphore_wait(barrier, groups + 2)

    moves = []
    for d in range(1, groups):
        to = peer(d)
        move = remote(
            grad_ref.at[to], landed.at[me], row_send.at[d], row_recv.at[d], (to, view)
        )
        move.start()
        moves.append(move)
    cameras[view] = camera_ref[...]
    for i, v in enumerate((beside, across, diagonal)):
        move = remote(
            cameras.at[view], cameras.at[view], cam_send.at[i], cam_recv.at[i], (me, v)
        )
        move.start()
        moves.append(move)
    landed[me] = grad_ref[me]
    for move in moves:
        move.wait_recv()

    def ship(kind, owner, m, v):
        block = every.at[owner, m]
        return remote(block, block, view_send.at[kind, m], view_recv.at[kind, m], (me, v))

    def forward(m):
        ship(1, view, m, across).wait_recv()
        ship(2, across, m, beside).start()

    for m in range(blocks):
        picked = pick_block(
            lambda f, r: landed[r // 8, f, pl.ds(r % 8, 1), :], index_ref[8 * m : 8 * m + 8, :], rows
        )
        for f in range(9):
            every[view, m, f] = picked[f]
        ship(0, view, m, beside).start()
        ship(1, view, m, across).start()
        if m >= 2:
            forward(m - 2)
    for m in range(blocks - 2, blocks):
        forward(m)

    def finish(m, carry):
        ship(0, view, m, beside).wait_recv()
        ship(2, across, m, beside).wait_recv()
        at = pl.ds(pl.multiple_of(8 * m, 8), 8)

        def store(i, value):
            out_ref[i, at, :] = value

        backproject_block(
            lambda i: params_ref[i, at, :],
            [unpack_camera(cameras[v]) for v in range(4)],
            [[every[v, m, f] for f in range(9)] for v in range(4)],
            lambda i: out_ref[i, at, :],
            store,
        )
        return carry

    lax.fori_loop(0, blocks, finish, 0)
    for move in moves:
        move.wait_send()
    for m in range(blocks):
        ship(0, view, m, beside).wait_send()
        ship(1, view, m, across).wait_send()
        ship(2, across, m, beside).wait_send()


def return_rows(grads, inverse, camera, params):
    groups = grads.shape[0]
    rows = params.shape[1]
    return pl.pallas_call(
        functools.partial(return_kernel, groups),
        in_specs=[VMEM] * 4,
        out_specs=VMEM,
        out_shape=jax.ShapeDtypeStruct(params.shape, F32),
        scratch_shapes=[
            pltpu.VMEM((groups, 9, 8, LANES), F32),
            pltpu.VMEM((4, rows // 8, 9, 8, LANES), F32),
            pltpu.VMEM((4, 8, LANES), F32),
            pltpu.SemaphoreType.DMA((groups,)),
            pltpu.SemaphoreType.DMA((groups,)),
            pltpu.SemaphoreType.DMA((3,)),
            pltpu.SemaphoreType.DMA((3,)),
            pltpu.SemaphoreType.DMA((3, rows // 8)),
            pltpu.SemaphoreType.DMA((3, rows // 8)),
        ],
        compiler_params=pltpu.CompilerParams(
            collective_id=1, has_side_effects=True, vmem_limit_bytes=32 * 1024 * 1024
        ),
        name="return",
    )(grads, inverse, camera, params)


def backproject(params, grads):
    views, total = grads.shape[0], grads.shape[1]
    blocks = params.shape[1] // 8
    spec = pl.BlockSpec((params.shape[0], 8, LANES), lambda i: (0, i, 0))
    return pl.pallas_call(
        functools.partial(backproject_kernel, views, blocks),
        grid=(blocks,),
        in_specs=[
            spec,
            pl.BlockSpec((views, total, 8, LANES), lambda i: (0, 0, 0, 0)),
        ],
        out_specs=spec,
        out_shape=jax.ShapeDtypeStruct(params.shape, F32),
        name="backproject",
    )(params, grads)


def split_two(value):
    high = value.astype(BF16)
    return high, (value - high.astype(F32)).astype(BF16)


def split_three(value):
    high = value.astype(BF16).astype(F32)
    rest = value - high
    middle = rest.astype(BF16).astype(F32)
    return high, middle, rest - middle


def pixel_basis():
    pixel = np.arange(256)
    x = (pixel % 16) - 7.5
    y = (pixel // 16) - 7.5
    return np.stack([np.ones(256), x, y, x * x, x * y, y * y])


def spread_matrix():
    basis = pixel_basis()
    matrix = np.zeros((32, 640), np.float32)
    for s in range(3):
        matrix[9 * s : 9 * s + 6, :256] = basis
        for h in range(3):
            matrix[9 * s + 6 + h, 256 + 128 * h : 384 + 128 * h] = 1.0
    return jnp.asarray(matrix, BF16)


def moment_matrix():
    matrix = np.zeros((256, LANES), np.float32)
    matrix[:, 96:102] = pixel_basis().T
    return jnp.asarray(matrix, BF16)


def local_conic(feature_ref, m, center_u, center_v):
    shift_u = (feature_ref[m, 0] - center_u) * HALF
    shift_v = (feature_ref[m, 1] - center_v) * HALF
    scale = 1.0 / (HALF * HALF)
    return shift_u, shift_v, [feature_ref[m, 2 + i] * scale for i in range(3)]


def composite_kernel(
    feature_ref,
    meta_ref,
    pixel_grad_ref,
    spread_ref,
    moment_ref,
    image_ref,
    out_ref,
    coef_ref,
    alpha_ref,
    color_ref,
    weight_ref,
    shade_ref,
    reduce_ref,
    stage_a,
    stage_b,
    sums_ref,
    moments_ref,
):
    blocks = feature_ref.shape[0]
    rows = 8 * blocks
    center_u = meta_ref[0:1, :]
    center_v = meta_ref[1:2, :]
    lengths = meta_ref[2:3, :]
    lane = lax.broadcasted_iota(jnp.int32, (8, LANES), 1)
    sub = lax.broadcasted_iota(jnp.int32, (8, LANES), 0)

    for m in range(blocks):
        su, sv, (ca, cb, cc) = local_conic(feature_ref, m, center_u, center_v)
        place = ((8 * m + sub) * 8 + lane // 16).astype(F32)
        alive = place < lengths
        lin_u = ca * su + cb * sv
        lin_v = cb * su + cc * sv
        const = feature_ref[m, 5] - 0.5 * (lin_u * su + lin_v * sv)
        coefs = [const, lin_u, lin_v, -0.5 * ca, -cb, -0.5 * cc]
        dead = [-1.0e30, 0.0, 0.0, 0.0, 0.0, 0.0]
        coefs = [jnp.where(alive, c * LOG2E, d) for c, d in zip(coefs, dead)]
        coefs += [feature_ref[m, 6 + h] for h in range(3)]
        for i in range(9):
            for s, part in enumerate(split_three(coefs[i])):
                coef_ref[8 * m : 8 * m + 8, 9 * s + i, :] = part
        for i in range(27, 32):
            coef_ref[8 * m : 8 * m + 8, i, :] = jnp.zeros((8, LANES), F32)

    grads = pixel_grad_ref[...]
    high = grads.astype(BF16).astype(F32)
    stacked = jnp.concatenate([high, grads - high, jnp.zeros((32, 256), F32)], axis=0)
    by_pixel = jnp.transpose(stacked).astype(BF16)
    reduce_ref[0:256, :] = by_pixel
    reduce_ref[256:512, :] = by_pixel
    reduce_ref[512:768, :] = moment_ref[...]
    reduce_ref[768:1024, :] = moment_ref[...]

    def expand(i, carry):
        left = jnp.concatenate(
            [jnp.transpose(coef_ref[4 * i + s]) for s in range(4)], axis=0
        ).astype(BF16)
        spread = jnp.dot(left, spread_ref[...], preferred_element_type=F32)
        at = pl.ds(pl.multiple_of(512 * i, 512), 512)
        alpha_ref[at, :] = spread[:, 0:256]
        color_ref[at, :] = spread[:, 256:640]
        return carry

    lax.fori_loop(0, rows // 4, expand, 0)

    parts = [(g, b) for g in range(2) for b in range(2)]
    pixel_grads = {
        (g, b, h): pixel_grad_ref[16 * h + 8 * g : 16 * h + 8 * g + 8, 128 * b : 128 * b + 128]
        for g, b in parts
        for h in range(3)
    }

    def forward(q, carry):
        left, totals = list(carry[0]), list(carry[1])
        for kk in range(8):
            for g in range(2):
                at = pl.ds(pl.multiple_of(128 * q + 16 * kk + 8 * g, 8), 8)
                colors = [color_ref[at, 128 * h : 128 * h + 128] for h in range(3)]
                for b in range(2):
                    n = 2 * g + b
                    cols = slice(128 * b, 128 * b + 128)
                    alpha = jnp.exp2(alpha_ref[at, cols])
                    weight = alpha * left[n]
                    left[n] = left[n] - weight
                    shade = colors[0] * pixel_grads[g, b, 0]
                    shade = shade + colors[1] * pixel_grads[g, b, 1]
                    shade = shade + colors[2] * pixel_grads[g, b, 2]
                    for h in range(3):
                        totals[3 * n + h] = totals[3 * n + h] + weight * colors[h]
                    alpha_ref[at, cols] = alpha
                    weight_ref[at, cols] = weight
                    shade_ref[at, cols] = shade
        return tuple(left), tuple(totals)

    one = jnp.ones((8, LANES), F32)
    zero = jnp.zeros((8, LANES), F32)
    _, totals = lax.fori_loop(0, rows, forward, ((one,) * 4, (zero,) * 12))
    for n, (g, b) in enumerate(parts):
        for h in range(3):
            image_ref[8 * g : 8 * g + 8, h, 128 * b : 128 * b + 128] = totals[3 * n + h]

    def sweep(q, behind, stage):
        behind = list(behind)
        for kk in reversed(range(8)):
            for b in range(2):
                cols = slice(128 * b, 128 * b + 128)
                weights, slopes = [], []
                for g in range(2):
                    n = 2 * g + b
                    at = pl.ds(pl.multiple_of(128 * q + 16 * kk + 8 * g, 8), 8)
                    weight = weight_ref[at, cols]
                    gap = shade_ref[at, cols] - behind[n]
                    weights.append(weight)
                    slopes.append(weight * gap)
                    behind[n] = behind[n] + alpha_ref[at, cols] * gap
                split = split_two(jnp.concatenate(weights, axis=0))
                split += split_two(jnp.concatenate(slopes, axis=0))
                for i in range(4):
                    stage[16 * kk : 16 * kk + 16, 256 * i + 128 * b : 256 * i + 128 * b + 128] = split[i]
        return tuple(behind)

    def reduce_stage(q, stage):
        at = pl.ds(pl.multiple_of(128 * q, 128), 128)
        sums_ref[at, :] = jnp.dot(stage[...], reduce_ref[...], preferred_element_type=F32)

    stage_b[...] = jnp.zeros_like(stage_b)

    def backward(i, behind):
        q = rows - 1 - 2 * i
        reduce_stage(q + 1, stage_b)
        behind = sweep(q, behind, stage_a)
        reduce_stage(q, stage_a)
        return sweep(q - 1, behind, stage_b)

    lax.fori_loop(0, rows // 2, backward, (zero,) * 4)
    reduce_stage(0, stage_b)

    own = lax.broadcasted_iota(jnp.int32, (16, LANES), 0) == (
        lax.broadcasted_iota(jnp.int32, (16, LANES), 1) % 16
    )

    def collect(m, carry):
        for s in range(8):
            q = 8 * m + s
            at = pl.ds(pl.multiple_of(128 * q, 128), 128)
            turned = jnp.transpose(sums_ref[at, :])
            for i in range(6):
                moments_ref[i, s : s + 1, :] = turned[96 + i : 97 + i]
            for h in range(3):
                both = turned[16 * h : 16 * h + 16] + turned[48 + 16 * h : 64 + 16 * h]
                moments_ref[6 + h, s : s + 1, :] = jnp.sum(
                    jnp.where(own, both, 0.0), axis=0, keepdims=True
                )
        su, sv, (ca, cb, cc) = local_conic(feature_ref, m, center_u, center_v)
        m0, mx, my, mxx, mxy, myy = [moments_ref[i] for i in range(6)]
        scale = 1.0 / (HALF * HALF)
        dev_u = mx - su * m0
        dev_v = my - sv * m0
        out_ref[m, 0] = HALF * (ca * dev_u + cb * dev_v)
        out_ref[m, 1] = HALF * (cb * dev_u + cc * dev_v)
        out_ref[m, 2] = -0.5 * scale * (mxx - su * (mx + dev_u))
        out_ref[m, 3] = -scale * (mxy - su * my - sv * dev_u)
        out_ref[m, 4] = -0.5 * scale * (myy - sv * (my + dev_v))
        out_ref[m, 5] = m0
        for h in range(3):
            out_ref[m, 6 + h] = moments_ref[6 + h]
        return carry

    lax.fori_loop(0, blocks, collect, 0)


def composite(features, meta, pixel_grad, tiles):
    blocks = features.shape[0]
    count = blocks * 8 * LANES
    return pl.pallas_call(
        composite_kernel,
        in_specs=[VMEM] * 5,
        out_specs=[VMEM] * 2,
        out_shape=[
            jax.ShapeDtypeStruct((tiles, 3, 256), F32),
            jax.ShapeDtypeStruct((blocks, 9, 8, LANES), F32),
        ],
        scratch_shapes=[
            pltpu.VMEM((8 * blocks, 32, LANES), F32),
            pltpu.VMEM((count, 256), F32),
            pltpu.VMEM((count, 384), F32),
            pltpu.VMEM((count, 256), F32),
            pltpu.VMEM((count, 256), F32),
            pltpu.VMEM((1024, LANES), BF16),
            pltpu.VMEM((128, 1024), BF16),
            pltpu.VMEM((128, 1024), BF16),
            pltpu.VMEM((count + 128, LANES), F32),
            pltpu.VMEM((9, 8, LANES), F32),
        ],
        compiler_params=pltpu.CompilerParams(vmem_limit_bytes=56 * 1024 * 1024),
        name="composite",
    )(features, meta, pixel_grad, spread_matrix(), moment_matrix())


def to_blocks(sent):
    groups, width, reps, _ = sent.shape
    if reps == 8:
        return sent
    rows = sent.transpose(0, 2, 1, 3).reshape(groups * reps // 8, 8, width, LANES)
    return rows.transpose(0, 2, 1, 3)


def from_blocks(blocked, groups, reps):
    if reps == 8:
        return blocked
    width = blocked.shape[1]
    rows = blocked.transpose(0, 2, 1, 3).reshape(groups, reps, width, LANES)
    return rows.transpose(0, 2, 1, 3)


def simple_call(kernel, shape, dtype, name, *args):
    return pl.pallas_call(
        kernel,
        in_specs=[VMEM] * len(args),
        out_specs=VMEM,
        out_shape=jax.ShapeDtypeStruct(shape, dtype),
        name=name,
    )(*args)


def exchange(sent):
    return lax.all_to_all(sent, "space", split_axis=0, concat_axis=0, tiled=True)


def per_device(
    views, gaussians, camera_table, view_camera, tile_plan, requests, tile_lists, tile_lengths, pixel_grad
):
    groups, cap = requests.shape[2:]
    reps = cap // LANES
    tiles, span = tile_lists.shape[1:]
    slots = gaussians.shape[1]
    rows = slots // LANES
    blocks = rows // 8

    chosen = (jnp.arange(camera_table.shape[0], dtype=jnp.int32) == view_camera[0]).astype(F32)
    camera = jnp.sum(camera_table * chosen[:, None], axis=0)
    camera = jnp.broadcast_to(camera[:, None], (8, LANES))
    params = gaussians.reshape(gaussians.shape[0], rows, LANES)

    base = jnp.arange(groups, dtype=jnp.int32)[:, None] * cap
    place = (tile_lists[0].T.reshape(groups, cap) - base).reshape(groups, reps, LANES)
    asked = requests[0, 0].reshape(groups, reps, LANES)
    fused = reps == 8 and rows == 8 * groups and views == 4
    if fused:
        arrived, inverse = request_rows(asked, place, params, camera)
    else:
        wanted = simple_call(order_kernel, place.shape, jnp.int32, "order", asked, place)
        incoming = exchange(wanted).reshape(groups * reps, LANES)
        features = project_all(params, camera)
        sent = simple_call(
            gather_kernel, (groups * reps // 8, 9, 8, LANES), F32, "gather", features, incoming
        )
        arrived = to_blocks(exchange(from_blocks(sent, groups, reps)))
        inverse = simple_call(invert_kernel, (rows, LANES), jnp.int32, "invert", incoming)

    plan = tile_plan[0]
    center_u = ((plan % 120 * 16 + 8).astype(F32) - 960.0) / HALF
    center_v = ((plan // 120 * 16 + 8).astype(F32) - 540.0) / HALF
    meta = jnp.stack([center_u, center_v, tile_lengths[0].astype(F32)])
    meta = jnp.tile(meta, (1, LANES // tiles))
    by_color = pixel_grad[0].transpose(1, 0, 2).reshape(3 * tiles, 256)
    image, row_grads = composite(arrived, meta, by_color, tiles)

    if fused:
        total = return_rows(row_grads, inverse, camera, params)
    else:
        returned = to_blocks(exchange(from_blocks(row_grads, groups, reps)))
        packed = simple_call(
            ungather_kernel, (9 * blocks + 1, 8, LANES), F32, "ungather", returned, inverse, camera
        )
        total = backproject(params, lax.all_gather(packed, "view"))
    return (image[None], total.reshape(gaussians.shape))


def solution(mesh):
    placed = (
        P(None, "space"),
        P(),
        P("view"),
        P("view", "space"),
        P("view", "space", None, None),
        P("view", "space", None),
        P("view", "space"),
        P("view", "space", None, None),
    )
    return jax.shard_map(
        functools.partial(per_device, mesh.shape["view"]),
        mesh=mesh,
        in_specs=placed,
        out_specs=(P("view", "space", None, None), P(None, "space")),
        check_vma=False,
    )
```

```python
import functools
import math

import jax
import jax.numpy as jnp
import numpy as np
from jax import lax
from jax.experimental import pallas as pl
from jax.experimental.pallas import tpu as pltpu
from jax.sharding import PartitionSpec as P

sh_zero = 0.28209479177387814
sh_one = 0.4886025119029199
sh_two = (
    1.0925484305920792,
    -1.0925484305920792,
    0.31539156525252005,
    -1.0925484305920792,
    0.5462742152960396,
)
sh_three = (
    -0.5900435899266435,
    2.890611442640554,
    -0.4570457994644658,
    0.3731763325901154,
    -0.4570457994644658,
    1.445305721320277,
    -0.5900435899266435,
)
dilation = 0.3 / 291600.0
LOG2E = math.log2(math.e)
HALF = 540.0
F32 = jnp.float32
BF16 = jnp.bfloat16
LANES = 128
VMEM = pl.BlockSpec(memory_space=pltpu.VMEM)


def quat_matrix(quat_w, quat_x, quat_y, quat_z):
    inv = 1.0 / jnp.sqrt(quat_w * quat_w + quat_x * quat_x + quat_y * quat_y + quat_z * quat_z)
    w, x, y, z = quat_w * inv, quat_x * inv, quat_y * inv, quat_z * inv
    return [
        [1.0 - 2.0 * (y * y + z * z), 2.0 * (x * y - w * z), 2.0 * (x * z + w * y)],
        [2.0 * (x * y + w * z), 1.0 - 2.0 * (x * x + z * z), 2.0 * (y * z - w * x)],
        [2.0 * (x * z - w * y), 2.0 * (y * z + w * x), 1.0 - 2.0 * (x * x + y * y)],
    ]


def sh_basis(dir_x, dir_y, dir_z):
    sq_x = dir_x * dir_x
    sq_y = dir_y * dir_y
    sq_z = dir_z * dir_z
    return [
        -sh_one * dir_y,
        sh_one * dir_z,
        -sh_one * dir_x,
        sh_two[0] * dir_x * dir_y,
        sh_two[1] * dir_y * dir_z,
        sh_two[2] * (2.0 * sq_z - sq_x - sq_y),
        sh_two[3] * dir_x * dir_z,
        sh_two[4] * (sq_x - sq_y),
        sh_three[0] * dir_y * (3.0 * sq_x - sq_y),
        sh_three[1] * dir_x * dir_y * dir_z,
        sh_three[2] * dir_y * (4.0 * sq_z - sq_x - sq_y),
        sh_three[3] * dir_z * (2.0 * sq_z - 3.0 * sq_x - 3.0 * sq_y),
        sh_three[4] * dir_x * (4.0 * sq_z - sq_x - sq_y),
        sh_three[5] * dir_z * (sq_x - sq_y),
        sh_three[6] * dir_x * (sq_x - 3.0 * sq_y),
    ]


def shape_axes(*params):
    scales = [jnp.exp(params[0]), jnp.exp(params[1]), jnp.exp(params[2])]
    own_rot = quat_matrix(*params[3:7])
    return [own_rot[i][k] * scales[k] for i in range(3) for k in range(3)]


def screen_conic(center, shaped, camera):
    view_rot, offset_cam, focal_len = camera
    in_camera = [
        sum((view_rot[i][j] * center[j] for j in range(3))) + offset_cam[i] for i in range(3)
    ]
    turned = [
        [sum((view_rot[i][j] * shaped[3 * j + k] for j in range(3))) for k in range(3)]
        for i in range(3)
    ]
    inv_depth = 1.0 / in_camera[2]
    scale = focal_len * inv_depth
    screen_u = scale * in_camera[0]
    screen_v = scale * in_camera[1]
    slope_u = screen_u * inv_depth
    slope_v = screen_v * inv_depth
    jac_u = [scale * turned[0][k] - slope_u * turned[2][k] for k in range(3)]
    jac_v = [scale * turned[1][k] - slope_v * turned[2][k] for k in range(3)]
    cov_uu = sum((jac_u[k] * jac_u[k] for k in range(3))) + dilation
    cov_uv = sum((jac_u[k] * jac_v[k] for k in range(3)))
    cov_vv = sum((jac_v[k] * jac_v[k] for k in range(3))) + dilation
    inv_det = 1.0 / (cov_uu * cov_vv - cov_uv * cov_uv)
    return [screen_u, screen_v, cov_vv * inv_det, -cov_uv * inv_det, cov_uu * inv_det]


def directional(center, camera):
    view_rot, offset_cam, _ = camera
    toward = [
        center[i] + sum((view_rot[j][i] * offset_cam[j] for j in range(3))) for i in range(3)
    ]
    inv = 1.0 / jnp.sqrt(toward[0] * toward[0] + toward[1] * toward[1] + toward[2] * toward[2])
    return sh_basis(toward[0] * inv, toward[1] * inv, toward[2] * inv)


def unpack_camera(rows):
    full = [jnp.broadcast_to(rows[i : i + 1], (8, LANES)) for i in range(8)]
    return (quat_matrix(*full[0:4]), full[4:7], full[7])


def project_block(load, camera):
    params = [load(i) for i in range(11)]
    feats = screen_conic(params[0:3], shape_axes(*params[3:10]), camera)
    logit = params[10]
    feats.append(jnp.minimum(logit, 0.0) - jnp.log1p(jnp.exp(-jnp.abs(logit))))
    basis = directional(params[0:3], camera)
    for h in range(3):
        total = 0.5 + sh_zero * load(11 + h)
        for k in range(1, 16):
            total = total + basis[k - 1] * load(11 + 3 * k + h)
        feats.append(total)
    return feats


def project_kernel(params_ref, camera_ref, out_ref):
    feats = project_block(lambda i: params_ref[i], unpack_camera(camera_ref[...]))
    for i in range(9):
        out_ref[i] = feats[i]


def project_all(params, camera):
    blocks = params.shape[1] // 8
    return pl.pallas_call(
        project_kernel,
        grid=(blocks,),
        in_specs=[
            pl.BlockSpec((params.shape[0], 8, LANES), lambda i: (0, i, 0)),
            pl.BlockSpec((8, LANES), lambda i: (0, 0)),
        ],
        out_specs=pl.BlockSpec((9, 8, LANES), lambda i: (0, i, 0)),
        out_shape=jax.ShapeDtypeStruct((9,) + params.shape[1:], F32),
        name="project",
    )(params, camera)


def lane_pick(rows, lanes):
    return jnp.take_along_axis(rows, lanes, axis=1, mode="promise_in_bounds")


def order_rows(requests, place):
    cap = place.shape[1]
    parts = []
    for c in range(cap // LANES):
        at = place[:, LANES * c : LANES * c + LANES] & (cap - 1)
        lanes = at & (LANES - 1)
        high = at >> 7
        result = jnp.zeros_like(at)
        for r in range(cap // LANES):
            picked = lane_pick(requests[:, LANES * r : LANES * r + LANES], lanes)
            result = jnp.where(high == r, picked, result)
        parts.append(result)
    return parts


def order_kernel(request_ref, place_ref, out_ref):
    for c, part in enumerate(order_rows(request_ref[...], place_ref[...])):
        out_ref[:, c, :] = part


def invert_rows(blocks):
    rows = 8 * len(blocks)
    high_iota = lax.broadcasted_iota(jnp.int32, (rows, 8 * LANES), 0)
    lane_iota = lax.broadcasted_iota(jnp.int32, (LANES, 8 * LANES), 0)
    column = lax.broadcasted_iota(jnp.int32, (1, 8 * LANES), 1)
    total = jnp.zeros((2 * rows, LANES), F32)
    for m, block in enumerate(blocks):
        flat = jnp.concatenate([block[s : s + 1] for s in range(8)], axis=1)
        hit = high_iota == (flat >> 7)
        row_value = ((column >> 7) + 8 * m).astype(F32)
        lane_value = (column & (LANES - 1)).astype(F32)
        left = jnp.concatenate(
            [jnp.where(hit, row_value, 0.0), jnp.where(hit, lane_value, 0.0)], axis=0
        ).astype(BF16)
        right = jnp.where(lane_iota == (flat & (LANES - 1)), 1.0, 0.0).astype(BF16)
        total = total + lax.dot_general(
            left, right, (((1,), (1,)), ((), ())), preferred_element_type=F32
        )
    return (total[:rows] * float(LANES) + total[rows:]).astype(jnp.int32)


def invert_kernel(index_ref, out_ref):
    rows = index_ref.shape[0]
    out_ref[...] = invert_rows([index_ref[8 * m : 8 * m + 8, :] for m in range(rows // 8)])


def pick_block(load_row, index, source_rows):
    lanes = index & (LANES - 1)
    high = index >> 7

    def step(r, totals):
        hit = high == r
        return tuple(
            jnp.where(hit, lane_pick(jnp.broadcast_to(load_row(f, r), (8, LANES)), lanes), totals[f])
            for f in range(9)
        )

    start = tuple(jnp.zeros((8, LANES), F32) for _ in range(9))
    return lax.fori_loop(0, source_rows, step, start, unroll=8)


def gather_kernel(feature_ref, index_ref, out_ref):
    rows = feature_ref.shape[1]

    def block(m, carry):
        index = index_ref[pl.ds(pl.multiple_of(8 * m, 8), 8), :]
        picked = pick_block(lambda f, r: feature_ref[f, pl.ds(r, 1), :], index, rows)
        for f in range(9):
            out_ref[m, f] = picked[f]
        return carry

    lax.fori_loop(0, index_ref.shape[0] // 8, block, 0)


def ungather_kernel(grad_ref, index_ref, camera_ref, out_ref):
    rows = index_ref.shape[0]
    blocks = rows // 8

    def block(m, carry):
        index = index_ref[pl.ds(pl.multiple_of(8 * m, 8), 8), :]
        picked = pick_block(
            lambda f, r: grad_ref[r // 8, f, pl.ds(r % 8, 1), :], index, rows
        )
        for f in range(9):
            out_ref[f * blocks + m] = picked[f]
        return carry

    lax.fori_loop(0, blocks, block, 0)
    out_ref[9 * blocks] = camera_ref[...]


def backproject_block(load, cameras, grads, store):
    center = [load(i) for i in range(3)]
    shaped, back_shape = jax.vjp(shape_axes, *[load(i) for i in range(3, 10)])
    kept = [0.0] * 12
    bases = []
    backs = []
    for v, camera in enumerate(cameras):
        _, back = jax.vjp(lambda c, s: screen_conic(c, s, camera), center, shaped)
        center_grads, shaped_grads = back(grads[v][0:5])
        shares = list(center_grads) + list(shaped_grads)
        kept = [t + share for t, share in zip(kept, shares)]
        basis, back_dir = jax.vjp(lambda *c: directional(list(c), camera), *center)
        bases.append(basis)
        backs.append(back_dir)
    views = range(len(cameras))
    basis_grads = [[] for _ in views]
    for k in range(16):
        for h in range(3):
            at = 11 + 3 * k + h
            if k == 0:
                store(at, sh_zero * sum(grads[v][6 + h] for v in views))
            else:
                store(at, sum(bases[v][k - 1] * grads[v][6 + h] for v in views))
        if k:
            loaded = [load(11 + 3 * k + h) for h in range(3)]
            for v in views:
                basis_grads[v].append(sum(loaded[h] * grads[v][6 + h] for h in range(3)))
    for v in views:
        for i, share in enumerate(backs[v](basis_grads[v])):
            kept[i] = kept[i] + share
    for i in range(3):
        store(i, kept[i])
    for i, share in enumerate(back_shape(kept[3:12])):
        store(3 + i, share)
    store(10, sum(grads[v][5] for v in views) * jax.nn.sigmoid(-load(10)))


def backproject_kernel(views, blocks, params_ref, grad_ref, out_ref):
    m = pl.program_id(0)

    def store(i, value):
        out_ref[i] = value

    backproject_block(
        lambda i: params_ref[i],
        [unpack_camera(grad_ref[v, 9 * blocks]) for v in range(views)],
        [[grad_ref[v, f * blocks + m] for f in range(9)] for v in range(views)],
        store,
    )


def remote(src, dst, send, recv, device):
    return pltpu.make_async_remote_copy(
        src_ref=src,
        dst_ref=dst,
        send_sem=send,
        recv_sem=recv,
        device_id=device,
        device_id_type=pl.DeviceIdType.MESH,
    )


def turn_block(wide_ref, m, block_ref):
    width = wide_ref.shape[0]
    for i in range(0, width, 8):
        top = min(i + 8, width)
        for c in range(8):
            cols = pl.ds(pl.multiple_of(1024 * m + LANES * c, LANES), LANES)
            block_ref[i:top, c, :] = wide_ref[i:top, cols]


def pick_camera(chosen, by_column):
    index = lax.broadcasted_iota(jnp.int32, by_column.shape, 1)
    entries = jnp.sum(jnp.where(index == chosen, by_column, 0.0), axis=1, keepdims=True)
    return jnp.broadcast_to(entries, (by_column.shape[0], LANES))


def request_kernel(
    groups,
    chosen_ref,
    request_ref,
    place_ref,
    params_ref,
    table_ref,
    arrived_ref,
    inverse_ref,
    camera_ref,
    params,
    wanted,
    incoming,
    features,
    outbox,
    ask_send,
    ask_recv,
    row_send,
    row_recv,
):
    me = lax.axis_index("space")
    view = lax.axis_index("view")
    rows = features.shape[1]

    def peer(d):
        return lax.rem(me + (d + groups), groups)

    barrier = pltpu.get_barrier_semaphore()
    for d in range(1, groups):
        pl.semaphore_signal(
            barrier, inc=1, device_id=(peer(d), view), device_id_type=pl.DeviceIdType.MESH
        )
    for c, part in enumerate(order_rows(request_ref[...], place_ref[...])):
        wanted[:, c, :] = part
    pl.semaphore_wait(barrier, groups - 1)

    asks = []
    for d in range(1, groups):
        to = peer(d)
        ask = remote(
            wanted.at[to], incoming.at[me], ask_send.at[d], ask_recv.at[d], (to, view)
        )
        ask.start()
        asks.append(ask)
    incoming[me] = wanted[me]

    picked_camera = pick_camera(chosen_ref[0], table_ref[...])
    camera_ref[...] = picked_camera
    camera = unpack_camera(picked_camera)

    def project(m, carry):
        at = pl.ds(pl.multiple_of(8 * m, 8), 8)
        turn_block(params_ref, m, params)
        feats = project_block(lambda i: params[i], camera)
        for i in range(9):
            features[i, at, :] = feats[i]
        return carry

    lax.fori_loop(0, rows // 8, project, 0)

    answers = []
    for d in range(groups):
        if d:
            asks[d - 1].wait_recv()
        to = peer(-d)
        picked = pick_block(lambda f, r: features[f, pl.ds(r, 1), :], incoming[to], rows)
        box = outbox.at[d] if d else arrived_ref.at[me]
        for f in range(9):
            box[f] = picked[f]
        if d:
            answer = remote(
                outbox.at[d], arrived_ref.at[me], row_send.at[d], row_recv.at[d], (to, view)
            )
            answer.start()
            answers.append(answer)
    inverse_ref[...] = invert_rows([incoming[s] for s in range(groups)])
    for ask in asks:
        ask.wait_send()
    for answer in answers:
        answer.wait()


def request_rows(chosen, requests, place, gaussians, table):
    groups = requests.shape[0]
    rows = gaussians.shape[1] // LANES
    return pl.pallas_call(
        functools.partial(request_kernel, groups),
        in_specs=[pl.BlockSpec(memory_space=pltpu.SMEM)] + [VMEM] * 4,
        out_specs=[VMEM] * 3,
        out_shape=[
            jax.ShapeDtypeStruct((groups, 9, 8, LANES), F32),
            jax.ShapeDtypeStruct((rows, LANES), jnp.int32),
            jax.ShapeDtypeStruct((8, LANES), F32),
        ],
        scratch_shapes=[
            pltpu.VMEM((gaussians.shape[0], 8, LANES), F32),
            pltpu.VMEM((groups, 8, LANES), jnp.int32),
            pltpu.VMEM((groups, 8, LANES), jnp.int32),
            pltpu.VMEM((9, rows, LANES), F32),
            pltpu.VMEM((groups, 9, 8, LANES), F32),
        ]
        + [pltpu.SemaphoreType.DMA((groups,))] * 4,
        compiler_params=pltpu.CompilerParams(
            collective_id=0, has_side_effects=True, vmem_limit_bytes=32 * 1024 * 1024
        ),
        name="request",
    )(chosen, requests, place, gaussians, table)


def return_kernel(
    groups,
    grad_ref,
    index_ref,
    camera_ref,
    params_ref,
    out_ref,
    params,
    result,
    landed,
    every,
    cameras,
    row_send,
    row_recv,
    cam_send,
    cam_recv,
    view_send,
    view_recv,
):
    me = lax.axis_index("space")
    view = lax.axis_index("view")
    core = lax.rem(view, 2)
    beside = view + 1 - 2 * core
    across = lax.rem(view + 2, 4)
    diagonal = lax.rem(beside + 2, 4)
    rows = index_ref.shape[0]
    blocks = rows // 8
    width = params_ref.shape[0]

    def peer(d):
        return lax.rem(me + (d + groups), groups)

    barrier = pltpu.get_barrier_semaphore()
    for device in [(peer(d), view) for d in range(1, groups)] + [
        (me, v) for v in (beside, across, diagonal)
    ]:
        pl.semaphore_signal(
            barrier, inc=1, device_id=device, device_id_type=pl.DeviceIdType.MESH
        )
    pl.semaphore_wait(barrier, groups + 2)

    moves = []
    for d in range(1, groups):
        to = peer(d)
        move = remote(
            grad_ref.at[to], landed.at[me], row_send.at[d], row_recv.at[d], (to, view)
        )
        move.start()
        moves.append(move)
    cameras[view] = camera_ref[...]
    for i, v in enumerate((beside, across, diagonal)):
        move = remote(
            cameras.at[view], cameras.at[view], cam_send.at[i], cam_recv.at[i], (me, v)
        )
        move.start()
        moves.append(move)
    landed[me] = grad_ref[me]
    for move in moves:
        move.wait_recv()

    def ship(kind, owner, m, v):
        block = every.at[owner, m]
        return remote(block, block, view_send.at[kind, m], view_recv.at[kind, m], (me, v))

    def forward(m):
        ship(1, view, m, across).wait_recv()
        ship(2, across, m, beside).start()

    for m in range(blocks):
        picked = pick_block(
            lambda f, r: landed[r // 8, f, pl.ds(r % 8, 1), :], index_ref[8 * m : 8 * m + 8, :], rows
        )
        for f in range(9):
            every[view, m, f] = picked[f]
        ship(0, view, m, beside).start()
        ship(1, view, m, across).start()
        if m >= 2:
            forward(m - 2)
    for m in range(blocks - 2, blocks):
        forward(m)

    def finish(m, carry):
        ship(0, view, m, beside).wait_recv()
        ship(2, across, m, beside).wait_recv()
        turn_block(params_ref, m, params)

        def store(i, value):
            result[i] = value

        backproject_block(
            lambda i: params[i],
            [unpack_camera(cameras[v]) for v in range(4)],
            [[every[v, m, f] for f in range(9)] for v in range(4)],
            store,
        )
        for i in range(0, width, 8):
            top = min(i + 8, width)
            for c in range(8):
                cols = pl.ds(pl.multiple_of(1024 * m + LANES * c, LANES), LANES)
                out_ref[i:top, cols] = result[i:top, c, :]
        return carry

    lax.fori_loop(0, blocks, finish, 0)
    for move in moves:
        move.wait_send()
    for m in range(blocks):
        ship(0, view, m, beside).wait_send()
        ship(1, view, m, across).wait_send()
        ship(2, across, m, beside).wait_send()


def return_rows(grads, inverse, camera, gaussians):
    groups = grads.shape[0]
    rows = gaussians.shape[1] // LANES
    return pl.pallas_call(
        functools.partial(return_kernel, groups),
        in_specs=[VMEM] * 4,
        out_specs=VMEM,
        out_shape=jax.ShapeDtypeStruct(gaussians.shape, F32),
        scratch_shapes=[
            pltpu.VMEM((gaussians.shape[0], 8, LANES), F32),
            pltpu.VMEM((gaussians.shape[0], 8, LANES), F32),
            pltpu.VMEM((groups, 9, 8, LANES), F32),
            pltpu.VMEM((4, rows // 8, 9, 8, LANES), F32),
            pltpu.VMEM((4, 8, LANES), F32),
            pltpu.SemaphoreType.DMA((groups,)),
            pltpu.SemaphoreType.DMA((groups,)),
            pltpu.SemaphoreType.DMA((3,)),
            pltpu.SemaphoreType.DMA((3,)),
            pltpu.SemaphoreType.DMA((3, rows // 8)),
            pltpu.SemaphoreType.DMA((3, rows // 8)),
        ],
        compiler_params=pltpu.CompilerParams(
            collective_id=1, has_side_effects=True, vmem_limit_bytes=32 * 1024 * 1024
        ),
        name="return",
    )(grads, inverse, camera, gaussians)


def backproject(params, grads):
    views, total = grads.shape[0], grads.shape[1]
    blocks = params.shape[1] // 8
    spec = pl.BlockSpec((params.shape[0], 8, LANES), lambda i: (0, i, 0))
    return pl.pallas_call(
        functools.partial(backproject_kernel, views, blocks),
        grid=(blocks,),
        in_specs=[
            spec,
            pl.BlockSpec((views, total, 8, LANES), lambda i: (0, 0, 0, 0)),
        ],
        out_specs=spec,
        out_shape=jax.ShapeDtypeStruct(params.shape, F32),
        name="backproject",
    )(params, grads)


def split_two(value):
    high = value.astype(BF16)
    return high, (value - high.astype(F32)).astype(BF16)


def split_three(value):
    high = value.astype(BF16).astype(F32)
    rest = value - high
    middle = rest.astype(BF16).astype(F32)
    return high, middle, rest - middle


def pixel_basis():
    pixel = np.arange(256)
    x = (pixel % 16) - 7.5
    y = (pixel // 16) - 7.5
    return np.stack([np.ones(256), x, y, x * x, x * y, y * y])


def spread_matrix():
    basis = pixel_basis()
    matrix = np.zeros((32, 640), np.float32)
    for s in range(3):
        matrix[9 * s : 9 * s + 6, :256] = basis
        for h in range(3):
            matrix[9 * s + 6 + h, 256 + 128 * h : 384 + 128 * h] = 1.0
    return jnp.asarray(matrix, BF16)


def moment_matrix():
    matrix = np.zeros((256, LANES), np.float32)
    matrix[:, 96:102] = pixel_basis().T
    return jnp.asarray(matrix, BF16)


def local_conic(feature_ref, m, center_u, center_v):
    shift_u = (feature_ref[m, 0] - center_u) * HALF
    shift_v = (feature_ref[m, 1] - center_v) * HALF
    scale = 1.0 / (HALF * HALF)
    return shift_u, shift_v, [feature_ref[m, 2 + i] * scale for i in range(3)]


def composite_kernel(
    feature_ref,
    plan_ref,
    length_ref,
    pixel_grad_ref,
    spread_ref,
    moment_ref,
    image_ref,
    out_ref,
    coef_ref,
    alpha_ref,
    color_ref,
    weight_ref,
    shade_ref,
    reduce_ref,
    stage_a,
    stage_b,
    sums_ref,
    moments_ref,
):
    blocks = feature_ref.shape[0]
    rows = 8 * blocks
    plan = plan_ref[...].astype(F32)
    tile_row = jnp.floor((plan + 0.5) * (1.0 / 120.0))
    tile_column = plan - 120.0 * tile_row
    copies = LANES // plan.shape[1]

    def on_lanes(value):
        return jnp.concatenate([value] * copies, axis=1)

    center_u = on_lanes((16.0 * tile_column + 8.0 - 960.0) / HALF)
    center_v = on_lanes((16.0 * tile_row + 8.0 - 540.0) / HALF)
    lengths = on_lanes(length_ref[...].astype(F32))
    lane = lax.broadcasted_iota(jnp.int32, (8, LANES), 1)
    sub = lax.broadcasted_iota(jnp.int32, (8, LANES), 0)

    for m in range(blocks):
        su, sv, (ca, cb, cc) = local_conic(feature_ref, m, center_u, center_v)
        place = ((8 * m + sub) * 8 + lane // 16).astype(F32)
        alive = place < lengths
        lin_u = ca * su + cb * sv
        lin_v = cb * su + cc * sv
        const = feature_ref[m, 5] - 0.5 * (lin_u * su + lin_v * sv)
        coefs = [const, lin_u, lin_v, -0.5 * ca, -cb, -0.5 * cc]
        dead = [-1.0e30, 0.0, 0.0, 0.0, 0.0, 0.0]
        coefs = [jnp.where(alive, c * LOG2E, d) for c, d in zip(coefs, dead)]
        coefs += [feature_ref[m, 6 + h] for h in range(3)]
        for i in range(9):
            for s, part in enumerate(split_three(coefs[i])):
                coef_ref[8 * m : 8 * m + 8, 9 * s + i, :] = part
        for i in range(27, 32):
            coef_ref[8 * m : 8 * m + 8, i, :] = jnp.zeros((8, LANES), F32)

    grads = pixel_grad_ref[...]
    high = grads.astype(BF16).astype(F32)
    stacked = jnp.concatenate([high, grads - high, jnp.zeros((32, 256), F32)], axis=0)
    by_pixel = jnp.transpose(stacked).astype(BF16)
    reduce_ref[0:256, :] = by_pixel
    reduce_ref[256:512, :] = by_pixel
    reduce_ref[512:768, :] = moment_ref[...]
    reduce_ref[768:1024, :] = moment_ref[...]

    def expand(i, carry):
        left = jnp.concatenate(
            [jnp.transpose(coef_ref[4 * i + s]) for s in range(4)], axis=0
        ).astype(BF16)
        spread = jnp.dot(left, spread_ref[...], preferred_element_type=F32)
        at = pl.ds(pl.multiple_of(512 * i, 512), 512)
        alpha_ref[at, :] = spread[:, 0:256]
        color_ref[at, :] = spread[:, 256:640]
        return carry

    lax.fori_loop(0, rows // 4, expand, 0)

    parts = [(g, b) for g in range(2) for b in range(2)]
    pixel_grads = {
        (g, b, h): pixel_grad_ref[16 * h + 8 * g : 16 * h + 8 * g + 8, 128 * b : 128 * b + 128]
        for g, b in parts
        for h in range(3)
    }

    def forward(q, carry):
        left, totals = list(carry[0]), list(carry[1])
        for kk in range(16):
            for g in range(2):
                at = pl.ds(pl.multiple_of(256 * q + 16 * kk + 8 * g, 8), 8)
                colors = [color_ref[at, 128 * h : 128 * h + 128] for h in range(3)]
                for b in range(2):
                    n = 2 * g + b
                    cols = slice(128 * b, 128 * b + 128)
                    alpha = jnp.exp2(alpha_ref[at, cols])
                    weight = alpha * left[n]
                    left[n] = left[n] - weight
                    shade = colors[0] * pixel_grads[g, b, 0]
                    shade = shade + colors[1] * pixel_grads[g, b, 1]
                    shade = shade + colors[2] * pixel_grads[g, b, 2]
                    for h in range(3):
                        totals[3 * n + h] = totals[3 * n + h] + weight * colors[h]
                    alpha_ref[at, cols] = alpha
                    weight_ref[at, cols] = weight
                    shade_ref[at, cols] = shade
        return tuple(left), tuple(totals)

    one = jnp.ones((8, LANES), F32)
    zero = jnp.zeros((8, LANES), F32)
    _, totals = lax.fori_loop(0, rows // 2, forward, ((one,) * 4, (zero,) * 12))
    for n, (g, b) in enumerate(parts):
        for h in range(3):
            image_ref[16 * h + 8 * g : 16 * h + 8 * g + 8, 128 * b : 128 * b + 128] = totals[3 * n + h]

    def sweep(q, behind, stage):
        behind = list(behind)
        for kk in reversed(range(16)):
            for b in range(2):
                cols = slice(128 * b, 128 * b + 128)
                weights, slopes = [], []
                for g in range(2):
                    n = 2 * g + b
                    at = pl.ds(pl.multiple_of(256 * q + 16 * kk + 8 * g, 8), 8)
                    weight = weight_ref[at, cols]
                    gap = shade_ref[at, cols] - behind[n]
                    weights.append(weight)
                    slopes.append(weight * gap)
                    behind[n] = behind[n] + alpha_ref[at, cols] * gap
                split = split_two(jnp.concatenate(weights, axis=0))
                split += split_two(jnp.concatenate(slopes, axis=0))
                for i in range(4):
                    stage[16 * kk : 16 * kk + 16, 256 * i + 128 * b : 256 * i + 128 * b + 128] = split[i]
        return tuple(behind)

    def reduce_stage(q, stage):
        at = pl.ds(pl.multiple_of(256 * q, 256), 256)
        sums_ref[at, :] = jnp.dot(stage[...], reduce_ref[...], preferred_element_type=F32)

    stage_b[...] = jnp.zeros_like(stage_b)

    def backward(i, behind):
        q = rows // 2 - 1 - 2 * i
        reduce_stage(q + 1, stage_b)
        behind = sweep(q, behind, stage_a)
        reduce_stage(q, stage_a)
        return sweep(q - 1, behind, stage_b)

    lax.fori_loop(0, rows // 4, backward, (zero,) * 4)
    reduce_stage(0, stage_b)

    own = lax.broadcasted_iota(jnp.int32, (16, LANES), 0) == (
        lax.broadcasted_iota(jnp.int32, (16, LANES), 1) % 16
    )

    def collect(m, carry):
        for s in range(8):
            q = 8 * m + s
            at = pl.ds(pl.multiple_of(128 * q, 128), 128)
            turned = jnp.transpose(sums_ref[at, :])
            for i in range(6):
                moments_ref[i, s : s + 1, :] = turned[96 + i : 97 + i]
            for h in range(3):
                both = turned[16 * h : 16 * h + 16] + turned[48 + 16 * h : 64 + 16 * h]
                moments_ref[6 + h, s : s + 1, :] = jnp.sum(
                    jnp.where(own, both, 0.0), axis=0, keepdims=True
                )
        su, sv, (ca, cb, cc) = local_conic(feature_ref, m, center_u, center_v)
        m0, mx, my, mxx, mxy, myy = [moments_ref[i] for i in range(6)]
        scale = 1.0 / (HALF * HALF)
        dev_u = mx - su * m0
        dev_v = my - sv * m0
        out_ref[m, 0] = HALF * (ca * dev_u + cb * dev_v)
        out_ref[m, 1] = HALF * (cb * dev_u + cc * dev_v)
        out_ref[m, 2] = -0.5 * scale * (mxx - su * (mx + dev_u))
        out_ref[m, 3] = -scale * (mxy - su * my - sv * dev_u)
        out_ref[m, 4] = -0.5 * scale * (myy - sv * (my + dev_v))
        out_ref[m, 5] = m0
        for h in range(3):
            out_ref[m, 6 + h] = moments_ref[6 + h]
        return carry

    lax.fori_loop(0, blocks, collect, 0)


def composite(features, plan, lengths, pixel_grad):
    blocks = features.shape[0]
    count = blocks * 8 * LANES
    return pl.pallas_call(
        composite_kernel,
        in_specs=[VMEM] * 6,
        out_specs=[VMEM] * 2,
        out_shape=[
            jax.ShapeDtypeStruct(pixel_grad.shape, F32),
            jax.ShapeDtypeStruct((blocks, 9, 8, LANES), F32),
        ],
        scratch_shapes=[
            pltpu.VMEM((8 * blocks, 32, LANES), F32),
            pltpu.VMEM((count, 256), F32),
            pltpu.VMEM((count, 384), F32),
            pltpu.VMEM((count, 256), F32),
            pltpu.VMEM((count, 256), F32),
            pltpu.VMEM((1024, LANES), BF16),
            pltpu.VMEM((256, 1024), BF16),
            pltpu.VMEM((256, 1024), BF16),
            pltpu.VMEM((count + 256, LANES), F32),
            pltpu.VMEM((9, 8, LANES), F32),
        ],
        compiler_params=pltpu.CompilerParams(vmem_limit_bytes=48 * 1024 * 1024),
        name="composite",
    )(features, plan, lengths, pixel_grad, spread_matrix(), moment_matrix())


def to_blocks(sent):
    groups, width, reps, _ = sent.shape
    if reps == 8:
        return sent
    rows = sent.transpose(0, 2, 1, 3).reshape(groups * reps // 8, 8, width, LANES)
    return rows.transpose(0, 2, 1, 3)


def from_blocks(blocked, groups, reps):
    if reps == 8:
        return blocked
    width = blocked.shape[1]
    rows = blocked.transpose(0, 2, 1, 3).reshape(groups, reps, width, LANES)
    return rows.transpose(0, 2, 1, 3)


def simple_call(kernel, shape, dtype, name, *args):
    return pl.pallas_call(
        kernel,
        in_specs=[VMEM] * len(args),
        out_specs=VMEM,
        out_shape=jax.ShapeDtypeStruct(shape, dtype),
        name=name,
    )(*args)


def exchange(sent):
    return lax.all_to_all(sent, "space", split_axis=0, concat_axis=0, tiled=True)


def per_device(
    views, gaussians, camera_table, view_camera, tile_plan, requests, tile_lists, tile_lengths, pixel_grad
):
    groups, cap = requests.shape[2:]
    reps = cap // LANES
    tiles, span = tile_lists.shape[1:]
    slots = gaussians.shape[1]
    rows = slots // LANES
    blocks = rows // 8

    place = tile_lists[0].T.reshape(groups, cap)
    asked = requests[0, 0]
    fused = reps == 8 and rows == 8 * groups and views == 4
    if fused:
        arrived, inverse, camera = request_rows(
            view_camera, asked, place, gaussians, camera_table.T
        )
    else:
        params = gaussians.reshape(gaussians.shape[0], rows, LANES)
        chosen = (jnp.arange(camera_table.shape[0], dtype=jnp.int32) == view_camera[0]).astype(F32)
        camera = jnp.sum(camera_table * chosen[:, None], axis=0)
        camera = jnp.broadcast_to(camera[:, None], (8, LANES))
        wanted = simple_call(
            order_kernel, (groups, reps, LANES), jnp.int32, "order", asked, place
        )
        incoming = exchange(wanted).reshape(groups * reps, LANES)
        features = project_all(params, camera)
        sent = simple_call(
            gather_kernel, (groups * reps // 8, 9, 8, LANES), F32, "gather", features, incoming
        )
        arrived = to_blocks(exchange(from_blocks(sent, groups, reps)))
        inverse = simple_call(invert_kernel, (rows, LANES), jnp.int32, "invert", incoming)

    by_color = pixel_grad[0].transpose(1, 0, 2).reshape(3 * tiles, 256)
    image, row_grads = composite(arrived, tile_plan, tile_lengths, by_color)
    image = image.reshape(3, tiles, 256).transpose(1, 0, 2)

    if fused:
        total = return_rows(row_grads, inverse, camera, gaussians)
    else:
        returned = to_blocks(exchange(from_blocks(row_grads, groups, reps)))
        packed = simple_call(
            ungather_kernel, (9 * blocks + 1, 8, LANES), F32, "ungather", returned, inverse, camera
        )
        total = backproject(params, lax.all_gather(packed, "view")).reshape(gaussians.shape)
    return (image[None], total)


def solution(mesh):
    placed = (
        P(None, "space"),
        P(),
        P("view"),
        P("view", "space"),
        P("view", "space", None, None),
        P("view", "space", None),
        P("view", "space"),
        P("view", "space", None, None),
    )
    return jax.shard_map(
        functools.partial(per_device, mesh.shape["view"]),
        mesh=mesh,
        in_specs=placed,
        out_specs=(P("view", "space", None, None), P(None, "space")),
        check_vma=False,
    )
```

```python
import functools
import math

import jax
import jax.numpy as jnp
import numpy as np
from jax import lax
from jax.experimental import pallas as pl
from jax.experimental.pallas import tpu as pltpu
from jax.sharding import PartitionSpec as P

sh_zero = 0.28209479177387814
sh_one = 0.4886025119029199
sh_two = (
    1.0925484305920792,
    -1.0925484305920792,
    0.31539156525252005,
    -1.0925484305920792,
    0.5462742152960396,
)
sh_three = (
    -0.5900435899266435,
    2.890611442640554,
    -0.4570457994644658,
    0.3731763325901154,
    -0.4570457994644658,
    1.445305721320277,
    -0.5900435899266435,
)
dilation = 0.3 / 291600.0
LOG2E = math.log2(math.e)
HALF = 540.0
F32 = jnp.float32
BF16 = jnp.bfloat16
LANES = 128
VMEM = pl.BlockSpec(memory_space=pltpu.VMEM)


def quat_matrix(quat_w, quat_x, quat_y, quat_z):
    inv = 1.0 / jnp.sqrt(quat_w * quat_w + quat_x * quat_x + quat_y * quat_y + quat_z * quat_z)
    w, x, y, z = quat_w * inv, quat_x * inv, quat_y * inv, quat_z * inv
    return [
        [1.0 - 2.0 * (y * y + z * z), 2.0 * (x * y - w * z), 2.0 * (x * z + w * y)],
        [2.0 * (x * y + w * z), 1.0 - 2.0 * (x * x + z * z), 2.0 * (y * z - w * x)],
        [2.0 * (x * z - w * y), 2.0 * (y * z + w * x), 1.0 - 2.0 * (x * x + y * y)],
    ]


def sh_basis(dir_x, dir_y, dir_z):
    sq_x = dir_x * dir_x
    sq_y = dir_y * dir_y
    sq_z = dir_z * dir_z
    return [
        -sh_one * dir_y,
        sh_one * dir_z,
        -sh_one * dir_x,
        sh_two[0] * dir_x * dir_y,
        sh_two[1] * dir_y * dir_z,
        sh_two[2] * (2.0 * sq_z - sq_x - sq_y),
        sh_two[3] * dir_x * dir_z,
        sh_two[4] * (sq_x - sq_y),
        sh_three[0] * dir_y * (3.0 * sq_x - sq_y),
        sh_three[1] * dir_x * dir_y * dir_z,
        sh_three[2] * dir_y * (4.0 * sq_z - sq_x - sq_y),
        sh_three[3] * dir_z * (2.0 * sq_z - 3.0 * sq_x - 3.0 * sq_y),
        sh_three[4] * dir_x * (4.0 * sq_z - sq_x - sq_y),
        sh_three[5] * dir_z * (sq_x - sq_y),
        sh_three[6] * dir_x * (sq_x - 3.0 * sq_y),
    ]


def shape_axes(*params):
    scales = [jnp.exp(params[0]), jnp.exp(params[1]), jnp.exp(params[2])]
    own_rot = quat_matrix(*params[3:7])
    return [own_rot[i][k] * scales[k] for i in range(3) for k in range(3)]


def screen_conic(center, shaped, camera):
    view_rot, offset_cam, focal_len = camera
    in_camera = [
        sum((view_rot[i][j] * center[j] for j in range(3))) + offset_cam[i] for i in range(3)
    ]
    turned = [
        [sum((view_rot[i][j] * shaped[3 * j + k] for j in range(3))) for k in range(3)]
        for i in range(3)
    ]
    inv_depth = 1.0 / in_camera[2]
    scale = focal_len * inv_depth
    screen_u = scale * in_camera[0]
    screen_v = scale * in_camera[1]
    slope_u = screen_u * inv_depth
    slope_v = screen_v * inv_depth
    jac_u = [scale * turned[0][k] - slope_u * turned[2][k] for k in range(3)]
    jac_v = [scale * turned[1][k] - slope_v * turned[2][k] for k in range(3)]
    cov_uu = sum((jac_u[k] * jac_u[k] for k in range(3))) + dilation
    cov_uv = sum((jac_u[k] * jac_v[k] for k in range(3)))
    cov_vv = sum((jac_v[k] * jac_v[k] for k in range(3))) + dilation
    inv_det = 1.0 / (cov_uu * cov_vv - cov_uv * cov_uv)
    return [screen_u, screen_v, cov_vv * inv_det, -cov_uv * inv_det, cov_uu * inv_det]


def directional(center, camera):
    view_rot, offset_cam, _ = camera
    toward = [
        center[i] + sum((view_rot[j][i] * offset_cam[j] for j in range(3))) for i in range(3)
    ]
    inv = 1.0 / jnp.sqrt(toward[0] * toward[0] + toward[1] * toward[1] + toward[2] * toward[2])
    return sh_basis(toward[0] * inv, toward[1] * inv, toward[2] * inv)


def unpack_camera(rows):
    full = [jnp.broadcast_to(rows[i : i + 1], (8, LANES)) for i in range(8)]
    return (quat_matrix(*full[0:4]), full[4:7], full[7])


def project_block(load, camera):
    params = [load(i) for i in range(11)]
    feats = screen_conic(params[0:3], shape_axes(*params[3:10]), camera)
    logit = params[10]
    feats.append(jnp.minimum(logit, 0.0) - jnp.log1p(jnp.exp(-jnp.abs(logit))))
    basis = directional(params[0:3], camera)
    for h in range(3):
        total = 0.5 + sh_zero * load(11 + h)
        for k in range(1, 16):
            total = total + basis[k - 1] * load(11 + 3 * k + h)
        feats.append(total)
    return feats


def project_kernel(params_ref, camera_ref, out_ref):
    feats = project_block(lambda i: params_ref[i], unpack_camera(camera_ref[...]))
    for i in range(9):
        out_ref[i] = feats[i]


def project_all(params, camera):
    blocks = params.shape[1] // 8
    return pl.pallas_call(
        project_kernel,
        grid=(blocks,),
        in_specs=[
            pl.BlockSpec((params.shape[0], 8, LANES), lambda i: (0, i, 0)),
            pl.BlockSpec((8, LANES), lambda i: (0, 0)),
        ],
        out_specs=pl.BlockSpec((9, 8, LANES), lambda i: (0, i, 0)),
        out_shape=jax.ShapeDtypeStruct((9,) + params.shape[1:], F32),
        name="project",
    )(params, camera)


def lane_pick(rows, lanes):
    return jnp.take_along_axis(rows, lanes, axis=1, mode="promise_in_bounds")


def order_rows(requests, place):
    cap = place.shape[1]
    parts = []
    for c in range(cap // LANES):
        at = place[:, LANES * c : LANES * c + LANES] & (cap - 1)
        lanes = at & (LANES - 1)
        high = at >> 7
        result = jnp.zeros_like(at)
        for r in range(cap // LANES):
            picked = lane_pick(requests[:, LANES * r : LANES * r + LANES], lanes)
            result = jnp.where(high == r, picked, result)
        parts.append(result)
    return parts


def order_kernel(request_ref, place_ref, out_ref):
    for c, part in enumerate(order_rows(request_ref[...], place_ref[...])):
        out_ref[:, c, :] = part


def invert_rows(blocks):
    rows = 8 * len(blocks)
    high_iota = lax.broadcasted_iota(jnp.int32, (rows, 8 * LANES), 0)
    lane_iota = lax.broadcasted_iota(jnp.int32, (LANES, 8 * LANES), 0)
    column = lax.broadcasted_iota(jnp.int32, (1, 8 * LANES), 1)
    total = jnp.zeros((2 * rows, LANES), F32)
    for m, block in enumerate(blocks):
        flat = jnp.concatenate([block[s : s + 1] for s in range(8)], axis=1)
        hit = high_iota == (flat >> 7)
        row_value = ((column >> 7) + 8 * m).astype(F32)
        lane_value = (column & (LANES - 1)).astype(F32)
        left = jnp.concatenate(
            [jnp.where(hit, row_value, 0.0), jnp.where(hit, lane_value, 0.0)], axis=0
        ).astype(BF16)
        right = jnp.where(lane_iota == (flat & (LANES - 1)), 1.0, 0.0).astype(BF16)
        total = total + lax.dot_general(
            left, right, (((1,), (1,)), ((), ())), preferred_element_type=F32
        )
    return (total[:rows] * float(LANES) + total[rows:]).astype(jnp.int32)


def invert_kernel(index_ref, out_ref):
    rows = index_ref.shape[0]
    out_ref[...] = invert_rows([index_ref[8 * m : 8 * m + 8, :] for m in range(rows // 8)])


def pick_block(load_row, index, source_rows):
    lanes = index & (LANES - 1)
    high = index >> 7

    def step(r, totals):
        hit = high == r
        return tuple(
            jnp.where(hit, lane_pick(jnp.broadcast_to(load_row(f, r), (8, LANES)), lanes), totals[f])
            for f in range(9)
        )

    start = tuple(jnp.zeros((8, LANES), F32) for _ in range(9))
    return lax.fori_loop(0, source_rows, step, start, unroll=8)


def fill_table(load, table_ref):
    for f in range(9):
        for s, part in enumerate(split_three(load(f))):
            turned = jnp.transpose(part)
            table_ref[64 * f : 64 * f + 64, 128 * s : 128 * s + 128] = jnp.concatenate(
                [turned[:64], turned[64:]], axis=1
            ).astype(BF16)


def table_pick(table_ref, index, store):
    high_iota = lax.broadcasted_iota(jnp.int32, (128, 256), 0)
    low_iota = lax.broadcasted_iota(jnp.int32, (64, 256), 0)
    for c in range(4):
        slot = jnp.concatenate([index[2 * c : 2 * c + 1], index[2 * c + 1 : 2 * c + 2]], axis=1)
        high = ((slot >> 6) & 1) * 64 + (slot >> 7)
        hit = jnp.where(high_iota == high, 1.0, 0.0).astype(BF16)
        found = jnp.dot(
            table_ref[...], jnp.concatenate([hit] * 3, axis=0), preferred_element_type=F32
        )
        own = low_iota == (slot & 63)
        for f in range(9):
            row = jnp.sum(
                jnp.where(own, found[64 * f : 64 * f + 64], 0.0), axis=0, keepdims=True
            )
            store(f, 2 * c, row[:, :LANES])
            store(f, 2 * c + 1, row[:, LANES:])


def gather_kernel(feature_ref, index_ref, out_ref):
    rows = feature_ref.shape[1]

    def block(m, carry):
        index = index_ref[pl.ds(pl.multiple_of(8 * m, 8), 8), :]
        picked = pick_block(lambda f, r: feature_ref[f, pl.ds(r, 1), :], index, rows)
        for f in range(9):
            out_ref[m, f] = picked[f]
        return carry

    lax.fori_loop(0, index_ref.shape[0] // 8, block, 0)


def ungather_kernel(grad_ref, index_ref, camera_ref, out_ref):
    rows = index_ref.shape[0]
    blocks = rows // 8

    def block(m, carry):
        index = index_ref[pl.ds(pl.multiple_of(8 * m, 8), 8), :]
        picked = pick_block(
            lambda f, r: grad_ref[r // 8, f, pl.ds(r % 8, 1), :], index, rows
        )
        for f in range(9):
            out_ref[f * blocks + m] = picked[f]
        return carry

    lax.fori_loop(0, blocks, block, 0)
    out_ref[9 * blocks] = camera_ref[...]


def backproject_block(load, cameras, grads, store):
    center = [load(i) for i in range(3)]
    shaped, back_shape = jax.vjp(shape_axes, *[load(i) for i in range(3, 10)])
    kept = [0.0] * 12
    bases = []
    backs = []
    for v, camera in enumerate(cameras):
        _, back = jax.vjp(lambda c, s: screen_conic(c, s, camera), center, shaped)
        center_grads, shaped_grads = back(grads[v][0:5])
        shares = list(center_grads) + list(shaped_grads)
        kept = [t + share for t, share in zip(kept, shares)]
        basis, back_dir = jax.vjp(lambda *c: directional(list(c), camera), *center)
        bases.append(basis)
        backs.append(back_dir)
    views = range(len(cameras))
    basis_grads = [[] for _ in views]
    for k in range(16):
        for h in range(3):
            at = 11 + 3 * k + h
            if k == 0:
                store(at, sh_zero * sum(grads[v][6 + h] for v in views))
            else:
                store(at, sum(bases[v][k - 1] * grads[v][6 + h] for v in views))
        if k:
            loaded = [load(11 + 3 * k + h) for h in range(3)]
            for v in views:
                basis_grads[v].append(sum(loaded[h] * grads[v][6 + h] for h in range(3)))
    for v in views:
        for i, share in enumerate(backs[v](basis_grads[v])):
            kept[i] = kept[i] + share
    for i in range(3):
        store(i, kept[i])
    for i, share in enumerate(back_shape(kept[3:12])):
        store(3 + i, share)
    store(10, sum(grads[v][5] for v in views) * jax.nn.sigmoid(-load(10)))


def backproject_kernel(views, blocks, params_ref, grad_ref, out_ref):
    m = pl.program_id(0)

    def store(i, value):
        out_ref[i] = value

    backproject_block(
        lambda i: params_ref[i],
        [unpack_camera(grad_ref[v, 9 * blocks]) for v in range(views)],
        [[grad_ref[v, f * blocks + m] for f in range(9)] for v in range(views)],
        store,
    )


def remote(src, dst, send, recv, device):
    return pltpu.make_async_remote_copy(
        src_ref=src,
        dst_ref=dst,
        send_sem=send,
        recv_sem=recv,
        device_id=device,
        device_id_type=pl.DeviceIdType.MESH,
    )


def turn_block(wide_ref, m, block_ref):
    width = wide_ref.shape[0]
    for i in range(0, width, 8):
        top = min(i + 8, width)
        for c in range(8):
            cols = pl.ds(pl.multiple_of(1024 * m + LANES * c, LANES), LANES)
            block_ref[i:top, c, :] = wide_ref[i:top, cols]


def pick_camera(chosen, by_column):
    index = lax.broadcasted_iota(jnp.int32, by_column.shape, 1)
    entries = jnp.sum(jnp.where(index == chosen, by_column, 0.0), axis=1, keepdims=True)
    return jnp.broadcast_to(entries, (by_column.shape[0], LANES))


def request_kernel(
    groups,
    chosen_ref,
    request_ref,
    place_ref,
    params_ref,
    table_ref,
    arrived_ref,
    inverse_ref,
    camera_ref,
    params,
    wanted,
    incoming,
    features,
    table,
    outbox,
    ask_send,
    ask_recv,
    row_send,
    row_recv,
):
    me = lax.axis_index("space")
    view = lax.axis_index("view")
    rows = features.shape[1]

    def peer(d):
        return lax.rem(me + (d + groups), groups)

    barrier = pltpu.get_barrier_semaphore()
    for d in range(1, groups):
        pl.semaphore_signal(
            barrier, inc=1, device_id=(peer(d), view), device_id_type=pl.DeviceIdType.MESH
        )
    for c, part in enumerate(order_rows(request_ref[...], place_ref[...])):
        wanted[:, c, :] = part
    pl.semaphore_wait(barrier, groups - 1)

    asks = []
    for d in range(1, groups):
        to = peer(d)
        ask = remote(
            wanted.at[to], incoming.at[me], ask_send.at[d], ask_recv.at[d], (to, view)
        )
        ask.start()
        asks.append(ask)
    incoming[me] = wanted[me]

    picked_camera = pick_camera(chosen_ref[0], table_ref[...])
    camera_ref[...] = picked_camera
    camera = unpack_camera(picked_camera)

    def project(m, carry):
        at = pl.ds(pl.multiple_of(8 * m, 8), 8)
        turn_block(params_ref, m, params)
        feats = project_block(lambda i: params[i], camera)
        for i in range(9):
            features[i, at, :] = feats[i]
        return carry

    lax.fori_loop(0, rows // 8, project, 0)

    fill_table(lambda f: features[f], table)

    def ask_of(d):
        to = peer(d)
        return remote(
            wanted.at[to], incoming.at[me], ask_send.at[d], ask_recv.at[d], (to, view)
        )

    def answer_of(d):
        return remote(
            outbox.at[d],
            arrived_ref.at[me],
            row_send.at[d],
            row_recv.at[d],
            (peer(-d), view),
        )

    def answer(d, carry):
        ask_of(d).wait_recv()

        def store(f, r, values):
            outbox[d, f, r : r + 1, :] = values

        table_pick(table, incoming[peer(-d)], store)
        answer_of(d).start()
        return carry

    lax.fori_loop(1, groups, answer, 0)

    def store_own(f, r, values):
        arrived_ref[me, f, r : r + 1, :] = values

    table_pick(table, incoming[me], store_own)
    inverse_ref[...] = invert_rows([incoming[s] for s in range(groups)])
    for ask in asks:
        ask.wait_send()
    for d in range(1, groups):
        answer_of(d).wait()


def request_rows(chosen, requests, place, gaussians, table):
    groups = requests.shape[0]
    rows = gaussians.shape[1] // LANES
    return pl.pallas_call(
        functools.partial(request_kernel, groups),
        in_specs=[pl.BlockSpec(memory_space=pltpu.SMEM)] + [VMEM] * 4,
        out_specs=[VMEM] * 3,
        out_shape=[
            jax.ShapeDtypeStruct((groups, 9, 8, LANES), F32),
            jax.ShapeDtypeStruct((rows, LANES), jnp.int32),
            jax.ShapeDtypeStruct((8, LANES), F32),
        ],
        scratch_shapes=[
            pltpu.VMEM((gaussians.shape[0], 8, LANES), F32),
            pltpu.VMEM((groups, 8, LANES), jnp.int32),
            pltpu.VMEM((groups, 8, LANES), jnp.int32),
            pltpu.VMEM((9, rows, LANES), F32),
            pltpu.VMEM((576, 384), BF16),
            pltpu.VMEM((groups, 9, 8, LANES), F32),
        ]
        + [pltpu.SemaphoreType.DMA((groups,))] * 4,
        compiler_params=pltpu.CompilerParams(
            collective_id=0, has_side_effects=True, vmem_limit_bytes=32 * 1024 * 1024
        ),
        name="request",
    )(chosen, requests, place, gaussians, table)


def return_kernel(
    groups,
    grad_ref,
    index_ref,
    camera_ref,
    params_ref,
    out_ref,
    params,
    result,
    table,
    landed,
    every,
    cameras,
    row_send,
    row_recv,
    cam_send,
    cam_recv,
    view_send,
    view_recv,
):
    me = lax.axis_index("space")
    view = lax.axis_index("view")
    core = lax.rem(view, 2)
    beside = view + 1 - 2 * core
    across = lax.rem(view + 2, 4)
    diagonal = lax.rem(beside + 2, 4)
    rows = index_ref.shape[0]
    blocks = rows // 8
    width = params_ref.shape[0]

    def peer(d):
        return lax.rem(me + (d + groups), groups)

    barrier = pltpu.get_barrier_semaphore()
    for device in [(peer(d), view) for d in range(1, groups)] + [
        (me, v) for v in (beside, across, diagonal)
    ]:
        pl.semaphore_signal(
            barrier, inc=1, device_id=device, device_id_type=pl.DeviceIdType.MESH
        )
    pl.semaphore_wait(barrier, groups + 2)

    moves = []
    for d in range(1, groups):
        to = peer(d)
        move = remote(
            grad_ref.at[to], landed.at[me], row_send.at[d], row_recv.at[d], (to, view)
        )
        move.start()
        moves.append(move)
    cameras[view] = camera_ref[...]
    for i, v in enumerate((beside, across, diagonal)):
        move = remote(
            cameras.at[view], cameras.at[view], cam_send.at[i], cam_recv.at[i], (me, v)
        )
        move.start()
        moves.append(move)
    landed[me] = grad_ref[me]
    for move in moves:
        move.wait_recv()

    def ship(kind, owner, m, v):
        block = every.at[owner, m]
        return remote(block, block, view_send.at[kind, m], view_recv.at[kind, m], (me, v))

    def forward(m):
        ship(1, view, m, across).wait_recv()
        ship(2, across, m, beside).start()

    fill_table(
        lambda f: jnp.concatenate([landed[o, f] for o in range(groups)], axis=0), table
    )

    def spread(m, carry):
        def store(f, r, values):
            every[view, m, f, r : r + 1, :] = values

        table_pick(table, index_ref[pl.ds(pl.multiple_of(8 * m, 8), 8), :], store)
        ship(0, view, m, beside).start()
        ship(1, view, m, across).start()

        @pl.when(m >= 2)
        def _():
            forward(m - 2)

        return carry

    lax.fori_loop(0, blocks, spread, 0)
    for m in range(blocks - 2, blocks):
        forward(m)

    def finish(m, carry):
        ship(0, view, m, beside).wait_recv()
        ship(2, across, m, beside).wait_recv()
        turn_block(params_ref, m, params)

        def store(i, value):
            result[i] = value

        backproject_block(
            lambda i: params[i],
            [unpack_camera(cameras[v]) for v in range(4)],
            [[every[v, m, f] for f in range(9)] for v in range(4)],
            store,
        )
        for i in range(0, width, 8):
            top = min(i + 8, width)
            for c in range(8):
                cols = pl.ds(pl.multiple_of(1024 * m + LANES * c, LANES), LANES)
                out_ref[i:top, cols] = result[i:top, c, :]
        return carry

    lax.fori_loop(0, blocks, finish, 0)
    for move in moves:
        move.wait_send()
    for m in range(blocks):
        ship(0, view, m, beside).wait_send()
        ship(1, view, m, across).wait_send()
        ship(2, across, m, beside).wait_send()


def return_rows(grads, inverse, camera, gaussians):
    groups = grads.shape[0]
    rows = gaussians.shape[1] // LANES
    return pl.pallas_call(
        functools.partial(return_kernel, groups),
        in_specs=[VMEM] * 4,
        out_specs=VMEM,
        out_shape=jax.ShapeDtypeStruct(gaussians.shape, F32),
        scratch_shapes=[
            pltpu.VMEM((gaussians.shape[0], 8, LANES), F32),
            pltpu.VMEM((gaussians.shape[0], 8, LANES), F32),
            pltpu.VMEM((576, 384), BF16),
            pltpu.VMEM((groups, 9, 8, LANES), F32),
            pltpu.VMEM((4, rows // 8, 9, 8, LANES), F32),
            pltpu.VMEM((4, 8, LANES), F32),
            pltpu.SemaphoreType.DMA((groups,)),
            pltpu.SemaphoreType.DMA((groups,)),
            pltpu.SemaphoreType.DMA((3,)),
            pltpu.SemaphoreType.DMA((3,)),
            pltpu.SemaphoreType.DMA((3, rows // 8)),
            pltpu.SemaphoreType.DMA((3, rows // 8)),
        ],
        compiler_params=pltpu.CompilerParams(
            collective_id=1, has_side_effects=True, vmem_limit_bytes=32 * 1024 * 1024
        ),
        name="return",
    )(grads, inverse, camera, gaussians)


def backproject(params, grads):
    views, total = grads.shape[0], grads.shape[1]
    blocks = params.shape[1] // 8
    spec = pl.BlockSpec((params.shape[0], 8, LANES), lambda i: (0, i, 0))
    return pl.pallas_call(
        functools.partial(backproject_kernel, views, blocks),
        grid=(blocks,),
        in_specs=[
            spec,
            pl.BlockSpec((views, total, 8, LANES), lambda i: (0, 0, 0, 0)),
        ],
        out_specs=spec,
        out_shape=jax.ShapeDtypeStruct(params.shape, F32),
        name="backproject",
    )(params, grads)


def split_two(value):
    high = value.astype(BF16)
    return high, (value - high.astype(F32)).astype(BF16)


def split_three(value):
    high = value.astype(BF16).astype(F32)
    rest = value - high
    middle = rest.astype(BF16).astype(F32)
    return high, middle, rest - middle


def pixel_basis():
    pixel = np.arange(256)
    x = (pixel % 16) - 7.5
    y = (pixel // 16) - 7.5
    return np.stack([np.ones(256), x, y, x * x, x * y, y * y])


def spread_matrix():
    basis = pixel_basis()
    matrix = np.zeros((32, 640), np.float32)
    for s in range(3):
        matrix[9 * s : 9 * s + 6, :256] = basis
        for h in range(3):
            matrix[9 * s + 6 + h, 256 + 128 * h : 384 + 128 * h] = 1.0
    return jnp.asarray(matrix, BF16)


def moment_matrix():
    matrix = np.zeros((256, LANES), np.float32)
    matrix[:, 96:102] = pixel_basis().T
    return jnp.asarray(matrix, BF16)


def local_conic(feature_ref, m, center_u, center_v):
    shift_u = (feature_ref[m, 0] - center_u) * HALF
    shift_v = (feature_ref[m, 1] - center_v) * HALF
    scale = 1.0 / (HALF * HALF)
    return shift_u, shift_v, [feature_ref[m, 2 + i] * scale for i in range(3)]


def composite_kernel(
    feature_ref,
    plan_ref,
    length_ref,
    pixel_grad_ref,
    spread_ref,
    moment_ref,
    image_ref,
    out_ref,
    coef_ref,
    alpha_ref,
    color_ref,
    weight_ref,
    shade_ref,
    reduce_ref,
    stage_a,
    stage_b,
    sums_ref,
    moments_ref,
):
    blocks = feature_ref.shape[0]
    rows = 8 * blocks
    plan = plan_ref[...].astype(F32)
    tile_row = jnp.floor((plan + 0.5) * (1.0 / 120.0))
    tile_column = plan - 120.0 * tile_row
    copies = LANES // plan.shape[1]

    def on_lanes(value):
        return jnp.concatenate([value] * copies, axis=1)

    center_u = on_lanes((16.0 * tile_column + 8.0 - 960.0) / HALF)
    center_v = on_lanes((16.0 * tile_row + 8.0 - 540.0) / HALF)
    lengths = on_lanes(length_ref[...].astype(F32))
    lane = lax.broadcasted_iota(jnp.int32, (8, LANES), 1)
    sub = lax.broadcasted_iota(jnp.int32, (8, LANES), 0)

    for m in range(blocks):
        su, sv, (ca, cb, cc) = local_conic(feature_ref, m, center_u, center_v)
        place = ((8 * m + sub) * 8 + lane // 16).astype(F32)
        alive = place < lengths
        lin_u = ca * su + cb * sv
        lin_v = cb * su + cc * sv
        const = feature_ref[m, 5] - 0.5 * (lin_u * su + lin_v * sv)
        coefs = [const, lin_u, lin_v, -0.5 * ca, -cb, -0.5 * cc]
        dead = [-1.0e30, 0.0, 0.0, 0.0, 0.0, 0.0]
        coefs = [jnp.where(alive, c * LOG2E, d) for c, d in zip(coefs, dead)]
        coefs += [feature_ref[m, 6 + h] for h in range(3)]
        for i in range(9):
            for s, part in enumerate(split_three(coefs[i])):
                coef_ref[8 * m : 8 * m + 8, 9 * s + i, :] = part
        for i in range(27, 32):
            coef_ref[8 * m : 8 * m + 8, i, :] = jnp.zeros((8, LANES), F32)

    grads = pixel_grad_ref[...]
    high = grads.astype(BF16).astype(F32)
    stacked = jnp.concatenate([high, grads - high, jnp.zeros((32, 256), F32)], axis=0)
    by_pixel = jnp.transpose(stacked).astype(BF16)
    reduce_ref[0:256, :] = by_pixel
    reduce_ref[256:512, :] = by_pixel
    reduce_ref[512:768, :] = moment_ref[...]
    reduce_ref[768:1024, :] = moment_ref[...]

    def expand(i, carry):
        left = jnp.concatenate(
            [jnp.transpose(coef_ref[4 * i + s]) for s in range(4)], axis=0
        ).astype(BF16)
        spread = jnp.dot(left, spread_ref[...], preferred_element_type=F32)
        at = pl.ds(pl.multiple_of(512 * i, 512), 512)
        alpha_ref[at, :] = spread[:, 0:256]
        color_ref[at, :] = spread[:, 256:640]
        return carry

    lax.fori_loop(0, rows // 4, expand, 0)

    parts = [(g, b) for g in range(2) for b in range(2)]
    pixel_grads = {
        (g, b, h): pixel_grad_ref[16 * h + 8 * g : 16 * h + 8 * g + 8, 128 * b : 128 * b + 128]
        for g, b in parts
        for h in range(3)
    }

    def forward(q, carry):
        left, totals = list(carry[0]), list(carry[1])
        for kk in range(16):
            for g in range(2):
                at = pl.ds(pl.multiple_of(256 * q + 16 * kk + 8 * g, 8), 8)
                colors = [color_ref[at, 128 * h : 128 * h + 128] for h in range(3)]
                for b in range(2):
                    n = 2 * g + b
                    cols = slice(128 * b, 128 * b + 128)
                    alpha = jnp.exp2(alpha_ref[at, cols])
                    weight = alpha * left[n]
                    left[n] = left[n] - weight
                    shade = colors[0] * pixel_grads[g, b, 0]
                    shade = shade + colors[1] * pixel_grads[g, b, 1]
                    shade = shade + colors[2] * pixel_grads[g, b, 2]
                    for h in range(3):
                        totals[3 * n + h] = totals[3 * n + h] + weight * colors[h]
                    alpha_ref[at, cols] = alpha
                    weight_ref[at, cols] = weight
                    shade_ref[at, cols] = shade
        return tuple(left), tuple(totals)

    one = jnp.ones((8, LANES), F32)
    zero = jnp.zeros((8, LANES), F32)
    _, totals = lax.fori_loop(0, rows // 2, forward, ((one,) * 4, (zero,) * 12))
    for n, (g, b) in enumerate(parts):
        for h in range(3):
            image_ref[16 * h + 8 * g : 16 * h + 8 * g + 8, 128 * b : 128 * b + 128] = totals[3 * n + h]

    def sweep(q, behind, stage):
        behind = list(behind)
        for kk in reversed(range(16)):
            for b in range(2):
                cols = slice(128 * b, 128 * b + 128)
                weights, slopes = [], []
                for g in range(2):
                    n = 2 * g + b
                    at = pl.ds(pl.multiple_of(256 * q + 16 * kk + 8 * g, 8), 8)
                    weight = weight_ref[at, cols]
                    gap = shade_ref[at, cols] - behind[n]
                    weights.append(weight)
                    slopes.append(weight * gap)
                    behind[n] = behind[n] + alpha_ref[at, cols] * gap
                split = split_two(jnp.concatenate(weights, axis=0))
                split += split_two(jnp.concatenate(slopes, axis=0))
                for i in range(4):
                    stage[16 * kk : 16 * kk + 16, 256 * i + 128 * b : 256 * i + 128 * b + 128] = split[i]
        return tuple(behind)

    def reduce_stage(q, stage):
        at = pl.ds(pl.multiple_of(256 * q, 256), 256)
        sums_ref[at, :] = jnp.dot(stage[...], reduce_ref[...], preferred_element_type=F32)

    stage_b[...] = jnp.zeros_like(stage_b)

    def backward(i, behind):
        q = rows // 2 - 1 - 2 * i
        reduce_stage(q + 1, stage_b)
        behind = sweep(q, behind, stage_a)
        reduce_stage(q, stage_a)
        return sweep(q - 1, behind, stage_b)

    lax.fori_loop(0, rows // 4, backward, (zero,) * 4)
    reduce_stage(0, stage_b)

    own = lax.broadcasted_iota(jnp.int32, (16, LANES), 0) == (
        lax.broadcasted_iota(jnp.int32, (16, LANES), 1) % 16
    )

    def collect(m, carry):
        for s in range(8):
            q = 8 * m + s
            at = pl.ds(pl.multiple_of(128 * q, 128), 128)
            turned = jnp.transpose(sums_ref[at, :])
            for i in range(6):
                moments_ref[i, s : s + 1, :] = turned[96 + i : 97 + i]
            for h in range(3):
                both = turned[16 * h : 16 * h + 16] + turned[48 + 16 * h : 64 + 16 * h]
                moments_ref[6 + h, s : s + 1, :] = jnp.sum(
                    jnp.where(own, both, 0.0), axis=0, keepdims=True
                )
        su, sv, (ca, cb, cc) = local_conic(feature_ref, m, center_u, center_v)
        m0, mx, my, mxx, mxy, myy = [moments_ref[i] for i in range(6)]
        scale = 1.0 / (HALF * HALF)
        dev_u = mx - su * m0
        dev_v = my - sv * m0
        out_ref[m, 0] = HALF * (ca * dev_u + cb * dev_v)
        out_ref[m, 1] = HALF * (cb * dev_u + cc * dev_v)
        out_ref[m, 2] = -0.5 * scale * (mxx - su * (mx + dev_u))
        out_ref[m, 3] = -scale * (mxy - su * my - sv * dev_u)
        out_ref[m, 4] = -0.5 * scale * (myy - sv * (my + dev_v))
        out_ref[m, 5] = m0
        for h in range(3):
            out_ref[m, 6 + h] = moments_ref[6 + h]
        return carry

    lax.fori_loop(0, blocks, collect, 0)


def composite(features, plan, lengths, pixel_grad):
    blocks = features.shape[0]
    count = blocks * 8 * LANES
    return pl.pallas_call(
        composite_kernel,
        in_specs=[VMEM] * 6,
        out_specs=[VMEM] * 2,
        out_shape=[
            jax.ShapeDtypeStruct(pixel_grad.shape, F32),
            jax.ShapeDtypeStruct((blocks, 9, 8, LANES), F32),
        ],
        scratch_shapes=[
            pltpu.VMEM((8 * blocks, 32, LANES), F32),
            pltpu.VMEM((count, 256), F32),
            pltpu.VMEM((count, 384), F32),
            pltpu.VMEM((count, 256), F32),
            pltpu.VMEM((count, 256), F32),
            pltpu.VMEM((1024, LANES), BF16),
            pltpu.VMEM((256, 1024), BF16),
            pltpu.VMEM((256, 1024), BF16),
            pltpu.VMEM((count + 256, LANES), F32),
            pltpu.VMEM((9, 8, LANES), F32),
        ],
        compiler_params=pltpu.CompilerParams(vmem_limit_bytes=48 * 1024 * 1024),
        name="composite",
    )(features, plan, lengths, pixel_grad, spread_matrix(), moment_matrix())


def to_blocks(sent):
    groups, width, reps, _ = sent.shape
    if reps == 8:
        return sent
    rows = sent.transpose(0, 2, 1, 3).reshape(groups * reps // 8, 8, width, LANES)
    return rows.transpose(0, 2, 1, 3)


def from_blocks(blocked, groups, reps):
    if reps == 8:
        return blocked
    width = blocked.shape[1]
    rows = blocked.transpose(0, 2, 1, 3).reshape(groups, reps, width, LANES)
    return rows.transpose(0, 2, 1, 3)


def simple_call(kernel, shape, dtype, name, *args):
    return pl.pallas_call(
        kernel,
        in_specs=[VMEM] * len(args),
        out_specs=VMEM,
        out_shape=jax.ShapeDtypeStruct(shape, dtype),
        name=name,
    )(*args)


def exchange(sent):
    return lax.all_to_all(sent, "space", split_axis=0, concat_axis=0, tiled=True)


def per_device(
    views, gaussians, camera_table, view_camera, tile_plan, requests, tile_lists, tile_lengths, pixel_grad
):
    groups, cap = requests.shape[2:]
    reps = cap // LANES
    tiles, span = tile_lists.shape[1:]
    slots = gaussians.shape[1]
    rows = slots // LANES
    blocks = rows // 8

    place = tile_lists[0].T.reshape(groups, cap)
    asked = requests[0, 0]
    fused = reps == 8 and rows == 64 and groups == 8 and views == 4
    if fused:
        arrived, inverse, camera = request_rows(
            view_camera, asked, place, gaussians, camera_table.T
        )
    else:
        params = gaussians.reshape(gaussians.shape[0], rows, LANES)
        chosen = (jnp.arange(camera_table.shape[0], dtype=jnp.int32) == view_camera[0]).astype(F32)
        camera = jnp.sum(camera_table * chosen[:, None], axis=0)
        camera = jnp.broadcast_to(camera[:, None], (8, LANES))
        wanted = simple_call(
            order_kernel, (groups, reps, LANES), jnp.int32, "order", asked, place
        )
        incoming = exchange(wanted).reshape(groups * reps, LANES)
        features = project_all(params, camera)
        sent = simple_call(
            gather_kernel, (groups * reps // 8, 9, 8, LANES), F32, "gather", features, incoming
        )
        arrived = to_blocks(exchange(from_blocks(sent, groups, reps)))
        inverse = simple_call(invert_kernel, (rows, LANES), jnp.int32, "invert", incoming)

    by_color = pixel_grad[0].transpose(1, 0, 2).reshape(3 * tiles, 256)
    image, row_grads = composite(arrived, tile_plan, tile_lengths, by_color)
    image = image.reshape(3, tiles, 256).transpose(1, 0, 2)

    if fused:
        total = return_rows(row_grads, inverse, camera, gaussians)
    else:
        returned = to_blocks(exchange(from_blocks(row_grads, groups, reps)))
        packed = simple_call(
            ungather_kernel, (9 * blocks + 1, 8, LANES), F32, "ungather", returned, inverse, camera
        )
        total = backproject(params, lax.all_gather(packed, "view")).reshape(gaussians.shape)
    return (image[None], total)


def solution(mesh):
    placed = (
        P(None, "space"),
        P(),
        P("view"),
        P("view", "space"),
        P("view", "space", None, None),
        P("view", "space", None),
        P("view", "space"),
        P("view", "space", None, None),
    )
    return jax.shard_map(
        functools.partial(per_device, mesh.shape["view"]),
        mesh=mesh,
        in_specs=placed,
        out_specs=(P("view", "space", None, None), P(None, "space")),
        check_vma=False,
    )
```

```python
import functools
import math

import jax
import jax.numpy as jnp
import numpy as np
from jax import lax
from jax.experimental import pallas as pl
from jax.experimental.pallas import tpu as pltpu
from jax.sharding import PartitionSpec as P

sh_zero = 0.28209479177387814
sh_one = 0.4886025119029199
sh_two = (
    1.0925484305920792,
    -1.0925484305920792,
    0.31539156525252005,
    -1.0925484305920792,
    0.5462742152960396,
)
sh_three = (
    -0.5900435899266435,
    2.890611442640554,
    -0.4570457994644658,
    0.3731763325901154,
    -0.4570457994644658,
    1.445305721320277,
    -0.5900435899266435,
)
dilation = 0.3 / 291600.0
LOG2E = math.log2(math.e)
HALF = 540.0
F32 = jnp.float32
BF16 = jnp.bfloat16
LANES = 128
VMEM = pl.BlockSpec(memory_space=pltpu.VMEM)


def quat_matrix(quat_w, quat_x, quat_y, quat_z):
    inv = 1.0 / jnp.sqrt(quat_w * quat_w + quat_x * quat_x + quat_y * quat_y + quat_z * quat_z)
    w, x, y, z = quat_w * inv, quat_x * inv, quat_y * inv, quat_z * inv
    return [
        [1.0 - 2.0 * (y * y + z * z), 2.0 * (x * y - w * z), 2.0 * (x * z + w * y)],
        [2.0 * (x * y + w * z), 1.0 - 2.0 * (x * x + z * z), 2.0 * (y * z - w * x)],
        [2.0 * (x * z - w * y), 2.0 * (y * z + w * x), 1.0 - 2.0 * (x * x + y * y)],
    ]


def sh_basis(dir_x, dir_y, dir_z):
    sq_x = dir_x * dir_x
    sq_y = dir_y * dir_y
    sq_z = dir_z * dir_z
    return [
        -sh_one * dir_y,
        sh_one * dir_z,
        -sh_one * dir_x,
        sh_two[0] * dir_x * dir_y,
        sh_two[1] * dir_y * dir_z,
        sh_two[2] * (2.0 * sq_z - sq_x - sq_y),
        sh_two[3] * dir_x * dir_z,
        sh_two[4] * (sq_x - sq_y),
        sh_three[0] * dir_y * (3.0 * sq_x - sq_y),
        sh_three[1] * dir_x * dir_y * dir_z,
        sh_three[2] * dir_y * (4.0 * sq_z - sq_x - sq_y),
        sh_three[3] * dir_z * (2.0 * sq_z - 3.0 * sq_x - 3.0 * sq_y),
        sh_three[4] * dir_x * (4.0 * sq_z - sq_x - sq_y),
        sh_three[5] * dir_z * (sq_x - sq_y),
        sh_three[6] * dir_x * (sq_x - 3.0 * sq_y),
    ]


def shape_axes(*params):
    scales = [jnp.exp(params[0]), jnp.exp(params[1]), jnp.exp(params[2])]
    own_rot = quat_matrix(*params[3:7])
    return [own_rot[i][k] * scales[k] for i in range(3) for k in range(3)]


def screen_conic(center, shaped, camera):
    view_rot, offset_cam, focal_len = camera
    in_camera = [
        sum((view_rot[i][j] * center[j] for j in range(3))) + offset_cam[i] for i in range(3)
    ]
    turned = [
        [sum((view_rot[i][j] * shaped[3 * j + k] for j in range(3))) for k in range(3)]
        for i in range(3)
    ]
    inv_depth = 1.0 / in_camera[2]
    scale = focal_len * inv_depth
    screen_u = scale * in_camera[0]
    screen_v = scale * in_camera[1]
    slope_u = screen_u * inv_depth
    slope_v = screen_v * inv_depth
    jac_u = [scale * turned[0][k] - slope_u * turned[2][k] for k in range(3)]
    jac_v = [scale * turned[1][k] - slope_v * turned[2][k] for k in range(3)]
    cov_uu = sum((jac_u[k] * jac_u[k] for k in range(3))) + dilation
    cov_uv = sum((jac_u[k] * jac_v[k] for k in range(3)))
    cov_vv = sum((jac_v[k] * jac_v[k] for k in range(3))) + dilation
    inv_det = 1.0 / (cov_uu * cov_vv - cov_uv * cov_uv)
    return [screen_u, screen_v, cov_vv * inv_det, -cov_uv * inv_det, cov_uu * inv_det]


def directional(center, camera):
    view_rot, offset_cam, _ = camera
    toward = [
        center[i] + sum((view_rot[j][i] * offset_cam[j] for j in range(3))) for i in range(3)
    ]
    inv = 1.0 / jnp.sqrt(toward[0] * toward[0] + toward[1] * toward[1] + toward[2] * toward[2])
    return sh_basis(toward[0] * inv, toward[1] * inv, toward[2] * inv)


def unpack_camera(rows):
    full = [jnp.broadcast_to(rows[i : i + 1], (8, LANES)) for i in range(8)]
    return (quat_matrix(*full[0:4]), full[4:7], full[7])


def project_block(load, camera):
    params = [load(i) for i in range(11)]
    feats = screen_conic(params[0:3], shape_axes(*params[3:10]), camera)
    logit = params[10]
    feats.append(jnp.minimum(logit, 0.0) - jnp.log1p(jnp.exp(-jnp.abs(logit))))
    basis = directional(params[0:3], camera)
    for h in range(3):
        total = 0.5 + sh_zero * load(11 + h)
        for k in range(1, 16):
            total = total + basis[k - 1] * load(11 + 3 * k + h)
        feats.append(total)
    return feats


def project_kernel(params_ref, camera_ref, out_ref):
    feats = project_block(lambda i: params_ref[i], unpack_camera(camera_ref[...]))
    for i in range(9):
        out_ref[i] = feats[i]


def project_all(params, camera):
    blocks = params.shape[1] // 8
    return pl.pallas_call(
        project_kernel,
        grid=(blocks,),
        in_specs=[
            pl.BlockSpec((params.shape[0], 8, LANES), lambda i: (0, i, 0)),
            pl.BlockSpec((8, LANES), lambda i: (0, 0)),
        ],
        out_specs=pl.BlockSpec((9, 8, LANES), lambda i: (0, i, 0)),
        out_shape=jax.ShapeDtypeStruct((9,) + params.shape[1:], F32),
        name="project",
    )(params, camera)


def lane_pick(rows, lanes):
    return jnp.take_along_axis(rows, lanes, axis=1, mode="promise_in_bounds")


def order_rows(requests, place):
    cap = place.shape[1]
    parts = []
    for c in range(cap // LANES):
        at = place[:, LANES * c : LANES * c + LANES] & (cap - 1)
        lanes = at & (LANES - 1)
        high = at >> 7
        result = jnp.zeros_like(at)
        for r in range(cap // LANES):
            picked = lane_pick(requests[:, LANES * r : LANES * r + LANES], lanes)
            result = jnp.where(high == r, picked, result)
        parts.append(result)
    return parts


def order_kernel(request_ref, place_ref, out_ref):
    for c, part in enumerate(order_rows(request_ref[...], place_ref[...])):
        out_ref[:, c, :] = part


def invert_rows(blocks):
    rows = 8 * len(blocks)
    high_iota = lax.broadcasted_iota(jnp.int32, (rows, 8 * LANES), 0)
    lane_iota = lax.broadcasted_iota(jnp.int32, (LANES, 8 * LANES), 0)
    column = lax.broadcasted_iota(jnp.int32, (1, 8 * LANES), 1)
    total = jnp.zeros((2 * rows, LANES), F32)
    for m, block in enumerate(blocks):
        flat = jnp.concatenate([block[s : s + 1] for s in range(8)], axis=1)
        hit = high_iota == (flat >> 7)
        row_value = ((column >> 7) + 8 * m).astype(F32)
        lane_value = (column & (LANES - 1)).astype(F32)
        left = jnp.concatenate(
            [jnp.where(hit, row_value, 0.0), jnp.where(hit, lane_value, 0.0)], axis=0
        ).astype(BF16)
        right = jnp.where(lane_iota == (flat & (LANES - 1)), 1.0, 0.0).astype(BF16)
        total = total + lax.dot_general(
            left, right, (((1,), (1,)), ((), ())), preferred_element_type=F32
        )
    return (total[:rows] * float(LANES) + total[rows:]).astype(jnp.int32)


def invert_kernel(index_ref, out_ref):
    rows = index_ref.shape[0]
    out_ref[...] = invert_rows([index_ref[8 * m : 8 * m + 8, :] for m in range(rows // 8)])


def pick_block(load_row, index, source_rows):
    lanes = index & (LANES - 1)
    high = index >> 7

    def step(r, totals):
        hit = high == r
        return tuple(
            jnp.where(hit, lane_pick(jnp.broadcast_to(load_row(f, r), (8, LANES)), lanes), totals[f])
            for f in range(9)
        )

    start = tuple(jnp.zeros((8, LANES), F32) for _ in range(9))
    return lax.fori_loop(0, source_rows, step, start, unroll=8)


def fill_table(load, table_ref):
    for f in range(9):
        for s, part in enumerate(split_three(load(f))):
            turned = jnp.transpose(part)
            table_ref[64 * f : 64 * f + 64, 128 * s : 128 * s + 128] = jnp.concatenate(
                [turned[:64], turned[64:]], axis=1
            ).astype(BF16)


def table_pick(table_ref, index, store):
    high_iota = lax.broadcasted_iota(jnp.int32, (128, 256), 0)
    low_iota = lax.broadcasted_iota(jnp.int32, (64, 256), 0)
    for c in range(4):
        slot = jnp.concatenate([index[2 * c : 2 * c + 1], index[2 * c + 1 : 2 * c + 2]], axis=1)
        high = ((slot >> 6) & 1) * 64 + (slot >> 7)
        hit = jnp.where(high_iota == high, 1.0, 0.0).astype(BF16)
        found = jnp.dot(
            table_ref[...], jnp.concatenate([hit] * 3, axis=0), preferred_element_type=F32
        )
        own = low_iota == (slot & 63)
        for f in range(9):
            row = jnp.sum(
                jnp.where(own, found[64 * f : 64 * f + 64], 0.0), axis=0, keepdims=True
            )
            store(f, 2 * c, row[:, :LANES])
            store(f, 2 * c + 1, row[:, LANES:])


def gather_kernel(feature_ref, index_ref, out_ref):
    rows = feature_ref.shape[1]

    def block(m, carry):
        index = index_ref[pl.ds(pl.multiple_of(8 * m, 8), 8), :]
        picked = pick_block(lambda f, r: feature_ref[f, pl.ds(r, 1), :], index, rows)
        for f in range(9):
            out_ref[m, f] = picked[f]
        return carry

    lax.fori_loop(0, index_ref.shape[0] // 8, block, 0)


def ungather_kernel(grad_ref, index_ref, camera_ref, out_ref):
    rows = index_ref.shape[0]
    blocks = rows // 8

    def block(m, carry):
        index = index_ref[pl.ds(pl.multiple_of(8 * m, 8), 8), :]
        picked = pick_block(
            lambda f, r: grad_ref[r // 8, f, pl.ds(r % 8, 1), :], index, rows
        )
        for f in range(9):
            out_ref[f * blocks + m] = picked[f]
        return carry

    lax.fori_loop(0, blocks, block, 0)
    out_ref[9 * blocks] = camera_ref[...]


def backproject_block(load, cameras, grads, store):
    center = [load(i) for i in range(3)]
    shaped, back_shape = jax.vjp(shape_axes, *[load(i) for i in range(3, 10)])
    kept = [0.0] * 12
    bases = []
    backs = []
    for v, camera in enumerate(cameras):
        _, back = jax.vjp(lambda c, s: screen_conic(c, s, camera), center, shaped)
        center_grads, shaped_grads = back(grads[v][0:5])
        shares = list(center_grads) + list(shaped_grads)
        kept = [t + share for t, share in zip(kept, shares)]
        basis, back_dir = jax.vjp(lambda *c: directional(list(c), camera), *center)
        bases.append(basis)
        backs.append(back_dir)
    views = range(len(cameras))
    basis_grads = [[] for _ in views]
    for k in range(16):
        for h in range(3):
            at = 11 + 3 * k + h
            if k == 0:
                store(at, sh_zero * sum(grads[v][6 + h] for v in views))
            else:
                store(at, sum(bases[v][k - 1] * grads[v][6 + h] for v in views))
        if k:
            loaded = [load(11 + 3 * k + h) for h in range(3)]
            for v in views:
                basis_grads[v].append(sum(loaded[h] * grads[v][6 + h] for h in range(3)))
    for v in views:
        for i, share in enumerate(backs[v](basis_grads[v])):
            kept[i] = kept[i] + share
    for i in range(3):
        store(i, kept[i])
    for i, share in enumerate(back_shape(kept[3:12])):
        store(3 + i, share)
    store(10, sum(grads[v][5] for v in views) * jax.nn.sigmoid(-load(10)))


def backproject_kernel(views, blocks, params_ref, grad_ref, out_ref):
    m = pl.program_id(0)

    def store(i, value):
        out_ref[i] = value

    backproject_block(
        lambda i: params_ref[i],
        [unpack_camera(grad_ref[v, 9 * blocks]) for v in range(views)],
        [[grad_ref[v, f * blocks + m] for f in range(9)] for v in range(views)],
        store,
    )


def remote(src, dst, send, recv, device):
    return pltpu.make_async_remote_copy(
        src_ref=src,
        dst_ref=dst,
        send_sem=send,
        recv_sem=recv,
        device_id=device,
        device_id_type=pl.DeviceIdType.MESH,
    )


def turn_block(wide_ref, m, block_ref):
    width = wide_ref.shape[0]
    for i in range(0, width, 8):
        top = min(i + 8, width)
        for c in range(8):
            cols = pl.ds(pl.multiple_of(1024 * m + LANES * c, LANES), LANES)
            block_ref[i:top, c, :] = wide_ref[i:top, cols]


def pick_camera(chosen, by_column):
    index = lax.broadcasted_iota(jnp.int32, by_column.shape, 1)
    entries = jnp.sum(jnp.where(index == chosen, by_column, 0.0), axis=1, keepdims=True)
    return jnp.broadcast_to(entries, (by_column.shape[0], LANES))


def request_kernel(
    groups,
    chosen_ref,
    request_ref,
    place_ref,
    params_ref,
    table_ref,
    arrived_ref,
    inverse_ref,
    camera_ref,
    params,
    wanted,
    incoming,
    features,
    table,
    outbox,
    ask_send,
    ask_recv,
    row_send,
    row_recv,
):
    me = lax.axis_index("space")
    view = lax.axis_index("view")
    rows = features.shape[1]

    def peer(d):
        return lax.rem(me + (d + groups), groups)

    barrier = pltpu.get_barrier_semaphore()
    for d in range(1, groups):
        pl.semaphore_signal(
            barrier, inc=1, device_id=(peer(d), view), device_id_type=pl.DeviceIdType.MESH
        )
    for c, part in enumerate(order_rows(request_ref[...], place_ref[...])):
        wanted[:, c, :] = part
    pl.semaphore_wait(barrier, groups - 1)

    asks = []
    for d in range(1, groups):
        to = peer(d)
        ask = remote(
            wanted.at[to], incoming.at[me], ask_send.at[d], ask_recv.at[d], (to, view)
        )
        ask.start()
        asks.append(ask)
    incoming[me] = wanted[me]

    picked_camera = pick_camera(chosen_ref[0], table_ref[...])
    camera_ref[...] = picked_camera
    camera = unpack_camera(picked_camera)

    def project(m, carry):
        at = pl.ds(pl.multiple_of(8 * m, 8), 8)
        turn_block(params_ref, m, params)
        feats = project_block(lambda i: params[i], camera)
        for i in range(9):
            features[i, at, :] = feats[i]
        return carry

    lax.fori_loop(0, rows // 8, project, 0)

    fill_table(lambda f: features[f], table)

    def ask_of(d):
        to = peer(d)
        return remote(
            wanted.at[to], incoming.at[me], ask_send.at[d], ask_recv.at[d], (to, view)
        )

    def answer_of(d):
        return remote(
            outbox.at[d],
            arrived_ref.at[me],
            row_send.at[d],
            row_recv.at[d],
            (peer(-d), view),
        )

    def answer(d, carry):
        ask_of(d).wait_recv()

        def store(f, r, values):
            outbox[d, f, r : r + 1, :] = values

        table_pick(table, incoming[peer(-d)], store)
        answer_of(d).start()
        return carry

    lax.fori_loop(1, groups, answer, 0)

    def store_own(f, r, values):
        arrived_ref[me, f, r : r + 1, :] = values

    table_pick(table, incoming[me], store_own)
    inverse_ref[...] = invert_rows([incoming[s] for s in range(groups)])
    for ask in asks:
        ask.wait_send()
    for d in range(1, groups):
        answer_of(d).wait()


def request_rows(chosen, requests, place, gaussians, table):
    groups = requests.shape[0]
    rows = gaussians.shape[1] // LANES
    return pl.pallas_call(
        functools.partial(request_kernel, groups),
        in_specs=[pl.BlockSpec(memory_space=pltpu.SMEM)] + [VMEM] * 4,
        out_specs=[VMEM] * 3,
        out_shape=[
            jax.ShapeDtypeStruct((groups, 9, 8, LANES), F32),
            jax.ShapeDtypeStruct((rows, LANES), jnp.int32),
            jax.ShapeDtypeStruct((8, LANES), F32),
        ],
        scratch_shapes=[
            pltpu.VMEM((gaussians.shape[0], 8, LANES), F32),
            pltpu.VMEM((groups, 8, LANES), jnp.int32),
            pltpu.VMEM((groups, 8, LANES), jnp.int32),
            pltpu.VMEM((9, rows, LANES), F32),
            pltpu.VMEM((576, 384), BF16),
            pltpu.VMEM((groups, 9, 8, LANES), F32),
        ]
        + [pltpu.SemaphoreType.DMA((groups,))] * 4,
        compiler_params=pltpu.CompilerParams(
            collective_id=0, has_side_effects=True, vmem_limit_bytes=32 * 1024 * 1024
        ),
        name="request",
    )(chosen, requests, place, gaussians, table)


def return_kernel(
    groups,
    grad_ref,
    index_ref,
    camera_ref,
    params_ref,
    out_ref,
    params,
    result,
    table,
    landed,
    every,
    cameras,
    row_send,
    row_recv,
    cam_send,
    cam_recv,
    view_send,
    view_recv,
):
    me = lax.axis_index("space")
    view = lax.axis_index("view")
    core = lax.rem(view, 2)
    beside = view + 1 - 2 * core
    across = lax.rem(view + 2, 4)
    diagonal = lax.rem(beside + 2, 4)
    rows = index_ref.shape[0]
    blocks = rows // 8
    width = params_ref.shape[0]

    def peer(d):
        return lax.rem(me + (d + groups), groups)

    barrier = pltpu.get_barrier_semaphore()
    for device in [(peer(d), view) for d in range(1, groups)] + [
        (me, v) for v in (beside, across, diagonal)
    ]:
        pl.semaphore_signal(
            barrier, inc=1, device_id=device, device_id_type=pl.DeviceIdType.MESH
        )
    pl.semaphore_wait(barrier, groups + 2)

    moves = []
    for d in range(1, groups):
        to = peer(d)
        move = remote(
            grad_ref.at[to], landed.at[me], row_send.at[d], row_recv.at[d], (to, view)
        )
        move.start()
        moves.append(move)
    cameras[view] = camera_ref[...]
    for i, v in enumerate((beside, across, diagonal)):
        move = remote(
            cameras.at[view], cameras.at[view], cam_send.at[i], cam_recv.at[i], (me, v)
        )
        move.start()
        moves.append(move)
    landed[me] = grad_ref[me]
    for move in moves:
        move.wait_recv()

    def ship(kind, owner, m, v):
        block = every.at[owner, m]
        return remote(block, block, view_send.at[kind, m], view_recv.at[kind, m], (me, v))

    def forward(m):
        ship(1, view, m, across).wait_recv()
        ship(2, across, m, beside).start()

    fill_table(
        lambda f: jnp.concatenate([landed[o, f] for o in range(groups)], axis=0), table
    )

    def spread(m, carry):
        def store(f, r, values):
            every[view, m, f, r : r + 1, :] = values

        table_pick(table, index_ref[pl.ds(pl.multiple_of(8 * m, 8), 8), :], store)
        ship(0, view, m, beside).start()
        ship(1, view, m, across).start()

        @pl.when(m >= 2)
        def _():
            forward(m - 2)

        return carry

    lax.fori_loop(0, blocks, spread, 0)
    for m in range(blocks - 2, blocks):
        forward(m)

    def finish(m, carry):
        ship(0, view, m, beside).wait_recv()
        ship(2, across, m, beside).wait_recv()
        turn_block(params_ref, m, params)

        def store(i, value):
            result[i] = value

        backproject_block(
            lambda i: params[i],
            [unpack_camera(cameras[v]) for v in range(4)],
            [[every[v, m, f] for f in range(9)] for v in range(4)],
            store,
        )
        for i in range(0, width, 8):
            top = min(i + 8, width)
            for c in range(8):
                cols = pl.ds(pl.multiple_of(1024 * m + LANES * c, LANES), LANES)
                out_ref[i:top, cols] = result[i:top, c, :]
        return carry

    lax.fori_loop(0, blocks, finish, 0)
    for move in moves:
        move.wait_send()
    for m in range(blocks):
        ship(0, view, m, beside).wait_send()
        ship(1, view, m, across).wait_send()
        ship(2, across, m, beside).wait_send()


def return_rows(grads, inverse, camera, gaussians):
    groups = grads.shape[0]
    rows = gaussians.shape[1] // LANES
    return pl.pallas_call(
        functools.partial(return_kernel, groups),
        in_specs=[VMEM] * 4,
        out_specs=VMEM,
        out_shape=jax.ShapeDtypeStruct(gaussians.shape, F32),
        scratch_shapes=[
            pltpu.VMEM((gaussians.shape[0], 8, LANES), F32),
            pltpu.VMEM((gaussians.shape[0], 8, LANES), F32),
            pltpu.VMEM((576, 384), BF16),
            pltpu.VMEM((groups, 9, 8, LANES), F32),
            pltpu.VMEM((4, rows // 8, 9, 8, LANES), F32),
            pltpu.VMEM((4, 8, LANES), F32),
            pltpu.SemaphoreType.DMA((groups,)),
            pltpu.SemaphoreType.DMA((groups,)),
            pltpu.SemaphoreType.DMA((3,)),
            pltpu.SemaphoreType.DMA((3,)),
            pltpu.SemaphoreType.DMA((3, rows // 8)),
            pltpu.SemaphoreType.DMA((3, rows // 8)),
        ],
        compiler_params=pltpu.CompilerParams(
            collective_id=1, has_side_effects=True, vmem_limit_bytes=32 * 1024 * 1024
        ),
        name="return",
    )(grads, inverse, camera, gaussians)


def backproject(params, grads):
    views, total = grads.shape[0], grads.shape[1]
    blocks = params.shape[1] // 8
    spec = pl.BlockSpec((params.shape[0], 8, LANES), lambda i: (0, i, 0))
    return pl.pallas_call(
        functools.partial(backproject_kernel, views, blocks),
        grid=(blocks,),
        in_specs=[
            spec,
            pl.BlockSpec((views, total, 8, LANES), lambda i: (0, 0, 0, 0)),
        ],
        out_specs=spec,
        out_shape=jax.ShapeDtypeStruct(params.shape, F32),
        name="backproject",
    )(params, grads)


def split_two(value):
    high = value.astype(BF16)
    return high, (value - high.astype(F32)).astype(BF16)


def split_three(value):
    high = value.astype(BF16).astype(F32)
    rest = value - high
    middle = rest.astype(BF16).astype(F32)
    return high, middle, rest - middle


def pixel_basis():
    pixel = np.arange(256)
    x = (pixel % 16) - 7.5
    y = (pixel // 16) - 7.5
    return np.stack([np.ones(256), x, y, x * x, x * y, y * y])


def spread_matrix():
    basis = pixel_basis()
    matrix = np.zeros((32, 640), np.float32)
    for s in range(3):
        matrix[9 * s : 9 * s + 6, :256] = basis
        for h in range(3):
            matrix[9 * s + 6 + h, 256 + 128 * h : 384 + 128 * h] = 1.0
    return jnp.asarray(matrix, BF16)


def moment_matrix():
    matrix = np.zeros((256, LANES), np.float32)
    matrix[:, 96:102] = pixel_basis().T
    return jnp.asarray(matrix, BF16)


def local_conic(feature_ref, m, center_u, center_v):
    shift_u = (feature_ref[m, 0] - center_u) * HALF
    shift_v = (feature_ref[m, 1] - center_v) * HALF
    scale = 1.0 / (HALF * HALF)
    return shift_u, shift_v, [feature_ref[m, 2 + i] * scale for i in range(3)]


def composite_kernel(
    feature_ref,
    plan_ref,
    length_ref,
    pixel_grad_ref,
    spread_ref,
    moment_ref,
    image_ref,
    out_ref,
    coef_ref,
    power_a,
    power_b,
    color_a,
    color_b,
    alpha_ref,
    weight_ref,
    shade_ref,
    reduce_ref,
    stage_a,
    stage_b,
    sums_ref,
    moments_ref,
):
    blocks = feature_ref.shape[0]
    rows = 8 * blocks
    plan = plan_ref[...].astype(F32)
    tile_row = jnp.floor((plan + 0.5) * (1.0 / 120.0))
    tile_column = plan - 120.0 * tile_row
    copies = LANES // plan.shape[1]

    def on_lanes(value):
        return jnp.concatenate([value] * copies, axis=1)

    center_u = on_lanes((16.0 * tile_column + 8.0 - 960.0) / HALF)
    center_v = on_lanes((16.0 * tile_row + 8.0 - 540.0) / HALF)
    lengths = on_lanes(length_ref[...].astype(F32))
    lane = lax.broadcasted_iota(jnp.int32, (8, LANES), 1)
    sub = lax.broadcasted_iota(jnp.int32, (8, LANES), 0)

    for m in range(blocks):
        su, sv, (ca, cb, cc) = local_conic(feature_ref, m, center_u, center_v)
        place = ((8 * m + sub) * 8 + lane // 16).astype(F32)
        alive = place < lengths
        lin_u = ca * su + cb * sv
        lin_v = cb * su + cc * sv
        const = feature_ref[m, 5] - 0.5 * (lin_u * su + lin_v * sv)
        coefs = [const, lin_u, lin_v, -0.5 * ca, -cb, -0.5 * cc]
        dead = [-1.0e30, 0.0, 0.0, 0.0, 0.0, 0.0]
        coefs = [jnp.where(alive, c * LOG2E, d) for c, d in zip(coefs, dead)]
        coefs += [feature_ref[m, 6 + h] for h in range(3)]
        for i in range(9):
            for s, part in enumerate(split_three(coefs[i])):
                coef_ref[8 * m : 8 * m + 8, 9 * s + i, :] = part
        for i in range(27, 32):
            coef_ref[8 * m : 8 * m + 8, i, :] = jnp.zeros((8, LANES), F32)

    grads = pixel_grad_ref[...]
    high = grads.astype(BF16).astype(F32)
    stacked = jnp.concatenate([high, grads - high, jnp.zeros((32, 256), F32)], axis=0)
    by_pixel = jnp.transpose(stacked).astype(BF16)
    reduce_ref[0:256, :] = by_pixel
    reduce_ref[256:512, :] = by_pixel
    reduce_ref[512:768, :] = moment_ref[...]
    reduce_ref[768:1024, :] = moment_ref[...]

    coef_ref[rows : rows + 2] = jnp.zeros((2, 32, LANES), F32)

    def expand(q, power, color):
        left = jnp.concatenate(
            [jnp.transpose(coef_ref[2 * q + s]) for s in range(2)], axis=0
        ).astype(BF16)
        spread = jnp.dot(left, spread_ref[...], preferred_element_type=F32)
        power[...] = spread[:, 0:256]
        color[...] = spread[:, 256:640]

    parts = [(g, b) for g in range(2) for b in range(2)]
    pixel_grads = {
        (g, b, h): pixel_grad_ref[16 * h + 8 * g : 16 * h + 8 * g + 8, 128 * b : 128 * b + 128]
        for g, b in parts
        for h in range(3)
    }

    def forward(q, carry, power, color):
        left, totals = list(carry[0]), list(carry[1])
        for kk in range(16):
            for g in range(2):
                at = pl.ds(pl.multiple_of(256 * q + 16 * kk + 8 * g, 8), 8)
                near = slice(16 * kk + 8 * g, 16 * kk + 8 * g + 8)
                colors = [color[near, 128 * h : 128 * h + 128] for h in range(3)]
                for b in range(2):
                    n = 2 * g + b
                    cols = slice(128 * b, 128 * b + 128)
                    alpha = jnp.exp2(power[near, cols])
                    weight = alpha * left[n]
                    left[n] = left[n] - weight
                    shade = colors[0] * pixel_grads[g, b, 0]
                    shade = shade + colors[1] * pixel_grads[g, b, 1]
                    shade = shade + colors[2] * pixel_grads[g, b, 2]
                    for h in range(3):
                        totals[3 * n + h] = totals[3 * n + h] + weight * colors[h]
                    alpha_ref[at, cols] = alpha
                    weight_ref[at, cols] = weight
                    shade_ref[at, cols] = shade
        return tuple(left), tuple(totals)

    one = jnp.ones((8, LANES), F32)
    zero = jnp.zeros((8, LANES), F32)
    expand(0, power_a, color_a)

    def two_forward(i, carry):
        expand(2 * i + 1, power_b, color_b)
        carry = forward(2 * i, carry, power_a, color_a)
        expand(2 * i + 2, power_a, color_a)
        return forward(2 * i + 1, carry, power_b, color_b)

    _, totals = lax.fori_loop(0, rows // 4, two_forward, ((one,) * 4, (zero,) * 12))
    for n, (g, b) in enumerate(parts):
        for h in range(3):
            image_ref[16 * h + 8 * g : 16 * h + 8 * g + 8, 128 * b : 128 * b + 128] = totals[3 * n + h]

    def sweep(q, behind, stage):
        behind = list(behind)
        for kk in reversed(range(16)):
            for b in range(2):
                cols = slice(128 * b, 128 * b + 128)
                weights, slopes = [], []
                for g in range(2):
                    n = 2 * g + b
                    at = pl.ds(pl.multiple_of(256 * q + 16 * kk + 8 * g, 8), 8)
                    weight = weight_ref[at, cols]
                    gap = shade_ref[at, cols] - behind[n]
                    weights.append(weight)
                    slopes.append(weight * gap)
                    behind[n] = behind[n] + alpha_ref[at, cols] * gap
                split = split_two(jnp.concatenate(weights, axis=0))
                split += split_two(jnp.concatenate(slopes, axis=0))
                for i in range(4):
                    stage[16 * kk : 16 * kk + 16, 256 * i + 128 * b : 256 * i + 128 * b + 128] = split[i]
        return tuple(behind)

    def reduce_stage(q, stage):
        at = pl.ds(pl.multiple_of(256 * q, 256), 256)
        sums_ref[at, :] = jnp.dot(stage[...], reduce_ref[...], preferred_element_type=F32)

    stage_b[...] = jnp.zeros_like(stage_b)

    def backward(i, behind):
        q = rows // 2 - 1 - 2 * i
        reduce_stage(q + 1, stage_b)
        behind = sweep(q, behind, stage_a)
        reduce_stage(q, stage_a)
        return sweep(q - 1, behind, stage_b)

    lax.fori_loop(0, rows // 4, backward, (zero,) * 4)
    reduce_stage(0, stage_b)

    own = lax.broadcasted_iota(jnp.int32, (16, LANES), 0) == (
        lax.broadcasted_iota(jnp.int32, (16, LANES), 1) % 16
    )

    def collect(m, carry):
        for s in range(8):
            q = 8 * m + s
            at = pl.ds(pl.multiple_of(128 * q, 128), 128)
            turned = jnp.transpose(sums_ref[at, :])
            for i in range(6):
                moments_ref[i, s : s + 1, :] = turned[96 + i : 97 + i]
            for h in range(3):
                both = turned[16 * h : 16 * h + 16] + turned[48 + 16 * h : 64 + 16 * h]
                moments_ref[6 + h, s : s + 1, :] = jnp.sum(
                    jnp.where(own, both, 0.0), axis=0, keepdims=True
                )
        su, sv, (ca, cb, cc) = local_conic(feature_ref, m, center_u, center_v)
        m0, mx, my, mxx, mxy, myy = [moments_ref[i] for i in range(6)]
        scale = 1.0 / (HALF * HALF)
        dev_u = mx - su * m0
        dev_v = my - sv * m0
        out_ref[m, 0] = HALF * (ca * dev_u + cb * dev_v)
        out_ref[m, 1] = HALF * (cb * dev_u + cc * dev_v)
        out_ref[m, 2] = -0.5 * scale * (mxx - su * (mx + dev_u))
        out_ref[m, 3] = -scale * (mxy - su * my - sv * dev_u)
        out_ref[m, 4] = -0.5 * scale * (myy - sv * (my + dev_v))
        out_ref[m, 5] = m0
        for h in range(3):
            out_ref[m, 6 + h] = moments_ref[6 + h]
        return carry

    lax.fori_loop(0, blocks, collect, 0)


def composite(features, plan, lengths, pixel_grad):
    blocks = features.shape[0]
    count = blocks * 8 * LANES
    return pl.pallas_call(
        composite_kernel,
        in_specs=[VMEM] * 6,
        out_specs=[VMEM] * 2,
        out_shape=[
            jax.ShapeDtypeStruct(pixel_grad.shape, F32),
            jax.ShapeDtypeStruct((blocks, 9, 8, LANES), F32),
        ],
        scratch_shapes=[
            pltpu.VMEM((8 * blocks + 2, 32, LANES), F32),
            pltpu.VMEM((256, 256), F32),
            pltpu.VMEM((256, 256), F32),
            pltpu.VMEM((256, 384), F32),
            pltpu.VMEM((256, 384), F32),
            pltpu.VMEM((count, 256), F32),
            pltpu.VMEM((count, 256), F32),
            pltpu.VMEM((count, 256), F32),
            pltpu.VMEM((1024, LANES), BF16),
            pltpu.VMEM((256, 1024), BF16),
            pltpu.VMEM((256, 1024), BF16),
            pltpu.VMEM((count + 256, LANES), F32),
            pltpu.VMEM((9, 8, LANES), F32),
        ],
        compiler_params=pltpu.CompilerParams(vmem_limit_bytes=48 * 1024 * 1024),
        name="composite",
    )(features, plan, lengths, pixel_grad, spread_matrix(), moment_matrix())


def to_blocks(sent):
    groups, width, reps, _ = sent.shape
    if reps == 8:
        return sent
    rows = sent.transpose(0, 2, 1, 3).reshape(groups * reps // 8, 8, width, LANES)
    return rows.transpose(0, 2, 1, 3)


def from_blocks(blocked, groups, reps):
    if reps == 8:
        return blocked
    width = blocked.shape[1]
    rows = blocked.transpose(0, 2, 1, 3).reshape(groups, reps, width, LANES)
    return rows.transpose(0, 2, 1, 3)


def simple_call(kernel, shape, dtype, name, *args):
    return pl.pallas_call(
        kernel,
        in_specs=[VMEM] * len(args),
        out_specs=VMEM,
        out_shape=jax.ShapeDtypeStruct(shape, dtype),
        name=name,
    )(*args)


def exchange(sent):
    return lax.all_to_all(sent, "space", split_axis=0, concat_axis=0, tiled=True)


def per_device(
    views, gaussians, camera_table, view_camera, tile_plan, requests, tile_lists, tile_lengths, pixel_grad
):
    groups, cap = requests.shape[2:]
    reps = cap // LANES
    tiles, span = tile_lists.shape[1:]
    slots = gaussians.shape[1]
    rows = slots // LANES
    blocks = rows // 8

    place = tile_lists[0].T.reshape(groups, cap)
    asked = requests[0, 0]
    fused = reps == 8 and rows == 64 and groups == 8 and views == 4
    if fused:
        arrived, inverse, camera = request_rows(
            view_camera, asked, place, gaussians, camera_table.T
        )
    else:
        params = gaussians.reshape(gaussians.shape[0], rows, LANES)
        chosen = (jnp.arange(camera_table.shape[0], dtype=jnp.int32) == view_camera[0]).astype(F32)
        camera = jnp.sum(camera_table * chosen[:, None], axis=0)
        camera = jnp.broadcast_to(camera[:, None], (8, LANES))
        wanted = simple_call(
            order_kernel, (groups, reps, LANES), jnp.int32, "order", asked, place
        )
        incoming = exchange(wanted).reshape(groups * reps, LANES)
        features = project_all(params, camera)
        sent = simple_call(
            gather_kernel, (groups * reps // 8, 9, 8, LANES), F32, "gather", features, incoming
        )
        arrived = to_blocks(exchange(from_blocks(sent, groups, reps)))
        inverse = simple_call(invert_kernel, (rows, LANES), jnp.int32, "invert", incoming)

    by_color = pixel_grad[0].transpose(1, 0, 2).reshape(3 * tiles, 256)
    image, row_grads = composite(arrived, tile_plan, tile_lengths, by_color)
    image = image.reshape(3, tiles, 256).transpose(1, 0, 2)

    if fused:
        total = return_rows(row_grads, inverse, camera, gaussians)
    else:
        returned = to_blocks(exchange(from_blocks(row_grads, groups, reps)))
        packed = simple_call(
            ungather_kernel, (9 * blocks + 1, 8, LANES), F32, "ungather", returned, inverse, camera
        )
        total = backproject(params, lax.all_gather(packed, "view")).reshape(gaussians.shape)
    return (image[None], total)


def solution(mesh):
    placed = (
        P(None, "space"),
        P(),
        P("view"),
        P("view", "space"),
        P("view", "space", None, None),
        P("view", "space", None),
        P("view", "space"),
        P("view", "space", None, None),
    )
    return jax.shard_map(
        functools.partial(per_device, mesh.shape["view"]),
        mesh=mesh,
        in_specs=placed,
        out_specs=(P("view", "space", None, None), P(None, "space")),
        check_vma=False,
    )
```
